32 devices in a mesh: groups: 2 (over x), dap: 16 (over z, y, core).
Axes of the slice: x: 2, y: 2, z: 4, core: 2. Of those that a mesh axis runs over, the one named last changes fastest.
Arguments:
- pair: float32 [128, 64, 128], P(('groups', 'dap')), parts along dimension 0, may hold values from -6 to 6
- residue_mask: int32 [128], P('groups'), parts along dimension 0, may hold values from 0 to 1, as said below
- norm_gain: float32 [2, 2, 128], replicated, may hold values from 0.1 to 1.9
- norm_bias: float32 [2, 2, 128], replicated, may hold values from -3 to 3
- edge_w: bfloat16 [2, 128, 640], replicated, may hold values from -0.5 to 0.5
- edge_bias: float32 [2, 640], replicated, may hold values from -3 to 3
- out_w: bfloat16 [2, 128, 128], replicated, may hold values from -0.5 to 0.5
- out_bias: float32 [2, 128], replicated, may hold values from -3 to 3
Outputs:
- updated: float32 [128, 64, 128], P(('groups', 'dap')), parts along dimension 0
The draws below stay inside these ranges and needn't reach their ends.
There are 2 independent parts, one for each index of `groups`. The reference program is written for one: setup_inputs(seed, part) draws one part's arguments, and reference() takes and returns one part's arrays. A program takes and returns all parts, laid end to end along the dimension named above; an argument that names none is the same for every part. Nothing has to cross between parts.
Inputs may be any that keep to these rules, and one draw needn't show every extreme that they name: `residue_mask`: residues 0 to some count of at least 32 are 1 and all later ones 0.
All inputs are finite; a program needn't handle non-finite values.
Results may differ from the reference program's by a relative error of at most 0.0023.
Values may be sent and summed in bfloat16 or wider, within the bound.
No kernel may reach another device: no remote copies, remote signals or barrier semaphores. Data moves between devices by JAX's collectives and lax.ppermute only.
A program may use at most 128 MiB of HBM per device.

```python
import jax
import jax.numpy as jnp
from jax import lax

C = 128
CH = 128
N = 64


def draw_residue_mask(key, part):
    key = jax.random.fold_in(key, 11)
    valid = jax.random.randint(key, (), N // 2, N + 1)
    return (jnp.arange(N, dtype=jnp.int32) < valid).astype(jnp.int32)


def levels(key, dims, cuts, low, largest):
    loudness, own = 1.0, jax.random.fold_in(key, 6)
    for dim, shards_of in cuts:
        steps = jnp.exp(jax.random.uniform(jax.random.fold_in(own, dim), (shards_of,), jnp.float32, low / len(cuts), largest / len(cuts)))
        loudness = loudness * jnp.repeat(steps, dims[dim] // shards_of).reshape([-1 if axis == dim else 1 for axis in range(len(dims))])
    return loudness


def scatter_about(stream_key, dims, deviation, limit, shards=(), kind=jnp.bfloat16):
    values = jax.random.normal(stream_key, dims, jnp.float32) * deviation
    if len(shards) > 0:
        values = levels(stream_key, dims, shards, -0.22, 0.18) * values
    return jnp.clip(values, min=-limit, max=limit).astype(kind)


def setup_inputs(seed: int = 0, part: int = 0) -> dict:
    streams_of = jax.random.split(jax.random.key(seed), 9)
    own_keys = jax.random.split(jax.random.fold_in(streams_of[8], part), 9)
    return {
        "pair": scatter_about(own_keys[0], (N, N, C), 1.0, 6.0, ((0, 16),), jnp.float32),
        "residue_mask": draw_residue_mask(jax.random.fold_in(jax.random.fold_in(streams_of[8], part), 71), part),
        "norm_gain": jnp.clip(1.0 + 0.18 * jax.random.normal(streams_of[2], (2, 2, C), jnp.float32), 0.1, 1.9),
        "norm_bias": scatter_about(streams_of[3], (2, 2, C), 0.5, 3.0, (), jnp.float32),
        "edge_w": scatter_about(streams_of[4], (2, C, 4 * CH + C), C ** -0.5, 0.5),
        "edge_bias": scatter_about(streams_of[5], (2, 4 * CH + C), 0.5, 3.0, (), jnp.float32),
        "out_w": scatter_about(streams_of[6], (2, CH, C), CH ** -0.5, 0.5),
        "out_bias": scatter_about(streams_of[7], (2, C), 0.5, 3.0, (), jnp.float32),
    }


def normalize(values, gain, shift):
    mean = lax.optimization_barrier(jnp.mean(values, axis=-1, keepdims=True))
    centered = values - mean
    spread = lax.optimization_barrier(jnp.mean(centered * centered, axis=-1, keepdims=True))
    return centered * lax.rsqrt(spread + 1e-05) * gain + shift

def triangle_update(block, mask_f, norm_gain, norm_bias, edge_w, edge_bias, out_w, out_bias, layer, incoming):
    side = block.shape[0]
    channels = block.shape[2]
    hidden_width = out_w.shape[1]
    normed = normalize(block, norm_gain[layer, 0], norm_bias[layer, 0]).astype(jnp.bfloat16)
    projected = jnp.dot(normed.reshape(side * side, channels), edge_w[layer], preferred_element_type=jnp.float32)
    projected = projected.reshape(side, side, -1) + edge_bias[layer]
    weight = (mask_f[:, None] * mask_f[None, :])[:, :, None]
    h = hidden_width
    left_edge = (weight * jax.nn.sigmoid(projected[..., :h]) * projected[..., h:2 * h]).astype(jnp.bfloat16)
    right_edge = (weight * jax.nn.sigmoid(projected[..., 2 * h:3 * h]) * projected[..., 3 * h:4 * h]).astype(jnp.bfloat16)
    gate_value = jax.nn.sigmoid(projected[..., 4 * h:])
    left_f = left_edge.astype(jnp.float32)
    right_f = right_edge.astype(jnp.float32)
    if incoming:
        contracted = jnp.einsum('kic,kjc->ijc', left_f, right_f)
    else:
        contracted = jnp.einsum('ikc,jkc->ijc', left_f, right_f)
    normed_out = normalize(contracted, norm_gain[layer, 1], norm_bias[layer, 1]).astype(jnp.bfloat16)
    result = jnp.dot(normed_out.reshape(side * side, hidden_width), out_w[layer], preferred_element_type=jnp.float32)
    result = result.reshape(side, side, channels) + out_bias[layer]
    return block + gate_value * result

def reference(pair, residue_mask, norm_gain, norm_bias, edge_w, edge_bias, out_w, out_bias):
    mask_f = residue_mask.astype(jnp.float32)
    first = triangle_update(pair, mask_f, norm_gain, norm_bias, edge_w, edge_bias, out_w, out_bias, 0, False)
    return triangle_update(first, mask_f, norm_gain, norm_bias, edge_w, edge_bias, out_w, out_bias, 1, True)
```

```python
import functools

import jax
import jax.numpy as jnp
from jax import lax
from jax.experimental import pallas as pl
from jax.experimental.pallas import tpu as pltpu
from jax.sharding import PartitionSpec as P

F32 = jnp.float32
BF16 = jnp.bfloat16
VMEM = pl.BlockSpec(memory_space=pltpu.VMEM)
SMEM = pl.BlockSpec(memory_space=pltpu.SMEM)


def normalize(values, gain, shift):
    mean = jnp.mean(values, axis=-1, keepdims=True)
    centered = values - mean
    spread = jnp.mean(centered * centered, axis=-1, keepdims=True)
    return centered * lax.rsqrt(spread + 1e-05) * gain + shift


def sigmoid(values):
    return 0.5 * jnp.tanh(0.5 * values) + 0.5


def edges(block, rows, first_row, mask_ref, gain_ref, shift_ref, edge_w_ref, edge_bias_ref, layer):
    total, width = block.shape
    side = total // rows
    normed = normalize(block, gain_ref[layer, 0:1, :], shift_ref[layer, 0:1, :]).astype(BF16)
    bias = edge_bias_ref[layer : layer + 1, :]
    hidden = (edge_bias_ref.shape[1] - width) // 4

    def part(index, size):
        low = index * hidden
        return (
            jnp.dot(normed, edge_w_ref[layer, :, low : low + size], preferred_element_type=F32)
            + bias[:, low : low + size]
        )

    valid = jnp.sum(mask_ref[...].astype(F32), axis=1, keepdims=True)
    column = lax.broadcasted_iota(jnp.int32, (rows, side, hidden), 1)
    row = lax.broadcasted_iota(jnp.int32, (rows, side, hidden), 0) + first_row
    keep = (jnp.maximum(column, row).astype(F32) < valid.reshape(1, 1, 1)).reshape(total, hidden)
    left = jnp.where(keep, sigmoid(part(0, hidden)) * part(1, hidden), 0.0)
    right = jnp.where(keep, sigmoid(part(2, hidden)) * part(3, hidden), 0.0)
    return left, right, sigmoid(part(4, width))


def finish(block, contracted, gate, gain_ref, shift_ref, out_w_ref, out_bias_ref, layer):
    normed = normalize(contracted, gain_ref[layer, 1:2, :], shift_ref[layer, 1:2, :]).astype(BF16)
    result = jnp.dot(normed, out_w_ref[layer], preferred_element_type=F32)
    return block + gate * (result + out_bias_ref[layer : layer + 1, :])


def first_kernel(
    at_ref, pair_ref, mask_ref, gain_ref, shift_ref, edge_w_ref, edge_bias_ref,
    send_ref, left_ref, gate_ref,
):
    rows, side, width = pair_ref.shape
    block = pair_ref[...].reshape(rows * side, width)
    left, right, gate = edges(
        block, rows, at_ref[0], mask_ref, gain_ref, shift_ref, edge_w_ref, edge_bias_ref, 0
    )
    right = right.astype(BF16)
    for chip in range(send_ref.shape[0]):
        send_ref[chip] = right
    left_ref[...] = left.astype(BF16)
    gate_ref[...] = gate


def fold(parts, sub):
    shift = 1
    while len(parts) > 1:
        low = (sub & shift) == 0
        parts = [
            jnp.where(low, a, b) + pltpu.roll(jnp.where(low, b, a), shift, 0)
            for a, b in zip(parts[0::2], parts[1::2])
        ]
        shift *= 2
    return parts[0]


def second_kernel(
    at_ref, own_ref, other_ref, left_ref, gate_ref, pair_ref, mask_ref, gain_ref, shift_ref,
    out_w_ref, out_bias_ref, edge_w_ref, edge_bias_ref,
    send_ref, gate_out_ref, first_ref,
    left_scr, x_scr,
):
    rows, side, width = pair_ref.shape
    chips = send_ref.shape[0]
    hidden = left_ref.shape[1]
    left_scr[...] = left_ref[...].astype(F32)
    sub = lax.broadcasted_iota(jnp.int32, (8, hidden), 0)
    core = at_ref[1]

    @pl.loop(0, chips)
    def _(chip):
        totals = [[] for _ in range(rows)]
        for half in (own_ref, other_ref):
            for a in range(rows):
                right = half[chip, a * side : (a + 1) * side, :].astype(F32)
                for i in range(rows):
                    product = left_scr[i * side : (i + 1) * side, :] * right
                    totals[i].append(jnp.sum(product.reshape(side // 8, 8, hidden), axis=0))
        for i in range(rows):
            x = fold(totals[i], sub)
            x = jnp.where(core == 0, x, pltpu.roll(x, rows, 0))
            at = pl.multiple_of(chip * 2 * rows, 2 * rows)
            x_scr[i, pl.ds(at, 2 * rows), :] = x

    block = pair_ref[...].reshape(rows * side, width)
    contracted = x_scr[...].reshape(rows * side, hidden)
    first = finish(
        block, contracted, gate_ref[...], gain_ref, shift_ref, out_w_ref, out_bias_ref, 0
    )
    first_ref[...] = first
    left, right, gate = edges(
        first, rows, at_ref[0], mask_ref, gain_ref, shift_ref, edge_w_ref, edge_bias_ref, 1
    )
    gate_out_ref[...] = gate
    right = right.astype(BF16)
    left = left.reshape(rows, chips, 2 * rows, hidden)
    for chip in range(chips):
        send_ref[chip, 0 : rows * side, :] = right
        send_ref[chip, rows * side :, :] = (
            left[:, chip].reshape(2 * rows * rows, hidden).astype(BF16)
        )


def third_kernel(
    at_ref, own_ref, other_ref, first_ref, gate_ref, gain_ref, shift_ref, out_w_ref, out_bias_ref,
    out_ref, left_scr,
):
    rows, side, width = out_ref.shape
    chips = own_ref.shape[0]
    hidden = own_ref.shape[2]
    core = at_ref[1]
    for h, half in enumerate((own_ref, other_ref)):
        left_scr[h] = half[:, rows * side :, :].astype(F32)

    def step(chip, totals):
        totals = list(totals)
        for h, half in enumerate((own_ref, other_ref)):
            for a in range(rows):
                right = half[chip, a * side : (a + 1) * side, :].astype(F32)
                for i in range(rows):
                    left = left_scr[h, chip, pl.ds(a * 2 * rows + core * rows + i, 1), :]
                    totals[i] = totals[i] + left * right
        return tuple(totals)

    zero = jnp.zeros((side, hidden), F32)
    totals = lax.fori_loop(0, chips, step, (zero,) * rows)
    for i in range(rows):
        here = slice(i * side, (i + 1) * side)
        out_ref[i] = finish(
            first_ref[here, :], totals[i], gate_ref[here, :],
            gain_ref, shift_ref, out_w_ref, out_bias_ref, 1,
        )


def body(pair, residue_mask, norm_gain, norm_bias, edge_w, edge_bias, out_w, out_bias):
    rows, side, width = pair.shape
    hidden = out_w.shape[1]
    dap = lax.axis_size("dap")
    chips = dap // 2
    me = lax.axis_index("dap")
    at = jnp.stack([me * rows, me % 2]).astype(jnp.int32)
    mask = residue_mask.reshape(1, side)
    same_core = [[core + 2 * chip for chip in range(chips)] for core in range(2)]
    flip = [(device, device ^ 1) for device in range(dap)]
    params = pltpu.CompilerParams(vmem_limit_bytes=48 * 1024 * 1024)
    count = rows * side
    shape = jax.ShapeDtypeStruct

    def spread(send):
        block = send.shape[1]
        flat = send.reshape(chips * block, hidden)
        own = lax.all_to_all(flat, "dap", 0, 0, axis_index_groups=same_core, tiled=True)
        other = lax.ppermute(own, "dap", flip)
        return own.reshape(chips, block, hidden), other.reshape(chips, block, hidden)

    send, left, gate = pl.pallas_call(
        first_kernel,
        in_specs=[SMEM, VMEM, VMEM, VMEM, VMEM, VMEM, VMEM],
        out_specs=[VMEM, VMEM, VMEM],
        out_shape=[
            shape((chips, count, hidden), BF16),
            shape((count, hidden), BF16),
            shape((count, width), F32),
        ],
        compiler_params=params,
        name="project_first",
    )(at, pair, mask, norm_gain, norm_bias, edge_w, edge_bias)
    own, other = spread(send)

    send, gate, first = pl.pallas_call(
        second_kernel,
        in_specs=[SMEM] + [VMEM] * 12,
        out_specs=[VMEM, VMEM, VMEM],
        out_shape=[
            shape((chips, count + 2 * rows * rows, hidden), BF16),
            shape((count, width), F32),
            shape((count, width), F32),
        ],
        scratch_shapes=[
            pltpu.VMEM((count, hidden), F32),
            pltpu.VMEM((rows, side, hidden), F32),
        ],
        compiler_params=params,
        name="contract_outgoing",
    )(at, own, other, left, gate, pair, mask, norm_gain, norm_bias, out_w, out_bias, edge_w, edge_bias)
    own, other = spread(send)

    return pl.pallas_call(
        third_kernel,
        in_specs=[SMEM] + [VMEM] * 8,
        out_specs=VMEM,
        out_shape=shape((rows, side, width), F32),
        scratch_shapes=[pltpu.VMEM((2, chips, 2 * rows * rows, hidden), F32)],
        compiler_params=params,
        name="contract_incoming",
    )(at, own, other, first, gate, norm_gain, norm_bias, out_w, out_bias)


def solution(mesh):
    in_specs = (P(("groups", "dap"), None, None), P("groups"), P(), P(), P(), P(), P(), P())
    out_specs = P(("groups", "dap"), None, None)
    return jax.shard_map(body, mesh=mesh, in_specs=in_specs, out_specs=out_specs, check_vma=False)
```

```python
import functools

import jax
import jax.numpy as jnp
from jax import lax
from jax.experimental import pallas as pl
from jax.experimental.pallas import tpu as pltpu
from jax.sharding import PartitionSpec as P

F32 = jnp.float32
BF16 = jnp.bfloat16
VMEM = pl.BlockSpec(memory_space=pltpu.VMEM)
SMEM = pl.BlockSpec(memory_space=pltpu.SMEM)
PLANE = 4
CHUNK = 64


def normalize(values, gain, shift):
    mean = jnp.mean(values, axis=-1, keepdims=True)
    centered = values - mean
    spread = jnp.mean(centered * centered, axis=-1, keepdims=True)
    return centered * lax.rsqrt(spread + 1e-05) * gain + shift


def sigmoid(values):
    return 0.5 * jnp.tanh(0.5 * values) + 0.5


def edges(block, rows, first_row, mask_ref, gain_ref, shift_ref, edge_w_ref, edge_bias_ref, layer):
    total, width = block.shape
    side = total // rows
    normed = normalize(block, gain_ref[layer, 0:1, :], shift_ref[layer, 0:1, :]).astype(BF16)
    bias = edge_bias_ref[layer : layer + 1, :]
    hidden = (edge_bias_ref.shape[1] - width) // 4

    def part(index, size):
        low = index * hidden
        return (
            jnp.dot(normed, edge_w_ref[layer, :, low : low + size], preferred_element_type=F32)
            + bias[:, low : low + size]
        )

    valid = jnp.sum(mask_ref[...].astype(F32), axis=1, keepdims=True)
    column = lax.broadcasted_iota(jnp.int32, (rows, side, hidden), 1)
    row = lax.broadcasted_iota(jnp.int32, (rows, side, hidden), 0) + first_row
    keep = (jnp.maximum(column, row).astype(F32) < valid.reshape(1, 1, 1)).reshape(total, hidden)
    left = jnp.where(keep, sigmoid(part(0, hidden)) * part(1, hidden), 0.0)
    right = jnp.where(keep, sigmoid(part(2, hidden)) * part(3, hidden), 0.0)
    return left, right, sigmoid(part(4, width))


def finish(block, contracted, gate, gain_ref, shift_ref, out_w_ref, out_bias_ref, layer):
    normed = normalize(contracted, gain_ref[layer, 1:2, :], shift_ref[layer, 1:2, :]).astype(BF16)
    result = jnp.dot(normed, out_w_ref[layer], preferred_element_type=F32)
    return block + gate * (result + out_bias_ref[layer : layer + 1, :])


def first_kernel(
    at_ref, pair_ref, mask_ref, gain_ref, shift_ref, edge_w_ref, edge_bias_ref,
    right_ref, left_ref, gate_ref,
):
    rows, side, width = pair_ref.shape
    block = pair_ref[...].reshape(rows * side, width)
    left, right, gate = edges(
        block, rows, at_ref[0] * rows, mask_ref, gain_ref, shift_ref, edge_w_ref, edge_bias_ref, 0
    )
    right_ref[...] = right.astype(BF16)
    left_ref[...] = left
    gate_ref[...] = gate


def fold(parts, sub):
    shift = 1
    while len(parts) > 1:
        low = (sub & shift) == 0
        parts = [
            jnp.where(low, a, b) + pltpu.roll(jnp.where(low, b, a), shift, 0)
            for a, b in zip(parts[0::2], parts[1::2])
        ]
        shift *= 2
    return parts[0]


def row_sums(left_ref, piece_ref, a, rows, side):
    hidden = left_ref.shape[1]

    def chunk(at, totals):
        right = piece_ref[pl.ds(a * side + at, CHUNK), :].astype(F32)
        sums = []
        for i in range(rows):
            product = left_ref[pl.ds(i * side + at, CHUNK), :] * right
            sums.append(jnp.sum(product.reshape(CHUNK // 8, 8, hidden), axis=0))
        return [t + s for t, s in zip(totals, sums)] if totals else sums

    totals = chunk(0, None)
    if side > CHUNK:
        totals = lax.fori_loop(
            1, side // CHUNK, lambda n, t: chunk(pl.multiple_of(n * CHUNK, CHUNK), t), totals
        )
    return totals


def second_kernel(pieces, at_ref, *refs):
    piece_refs = refs[:pieces]
    (
        left_ref, gate_ref, pair_ref, mask_ref, gain_ref, shift_ref,
        out_w_ref, out_bias_ref, edge_w_ref, edge_bias_ref,
    ) = refs[pieces : pieces + 10]
    outs = refs[pieces + 10 :]
    send_refs, (gate_out_ref, first_ref, x_scr, left_scr) = outs[:-4], outs[-4:]
    rows, side, width = pair_ref.shape
    hidden = left_ref.shape[1]
    sub = lax.broadcasted_iota(jnp.int32, (8, hidden), 0)
    me = at_ref[0]
    core = me & 1
    for s in range(0, pieces, 2):
        totals = [[] for _ in range(rows)]
        for piece in piece_refs[s : s + 2]:
            for a in range(rows):
                for i, total in enumerate(row_sums(left_ref, piece, a, rows, side)):
                    totals[i].append(total)
        at = pl.multiple_of((me >> 1 ^ s >> 1) * 2 * rows, 2 * rows)
        for i in range(rows):
            x = fold(totals[i], sub)
            x_scr[i, pl.ds(at, 2 * rows), :] = jnp.where(core == 0, x, pltpu.roll(x, rows, 0))

    block = pair_ref[...].reshape(rows * side, width)
    contracted = x_scr[...].reshape(rows * side, hidden)
    first = finish(
        block, contracted, gate_ref[...], gain_ref, shift_ref, out_w_ref, out_bias_ref, 0
    )
    first_ref[...] = first
    left, right, gate = edges(
        first, rows, me * rows, mask_ref, gain_ref, shift_ref, edge_w_ref, edge_bias_ref, 1
    )
    gate_out_ref[...] = gate
    left_scr[...] = left.reshape(rows, side, hidden)
    right = right.astype(BF16)
    near = PLANE * rows
    for k, send_ref in enumerate(send_refs):
        send_ref[0 : rows * side, :] = right
        at = pl.multiple_of((me // PLANE ^ k) * near, near)
        block = left_scr[:, pl.ds(at, near), :].reshape(rows * near, hidden)
        send_ref[rows * side :, :] = block.astype(BF16)


def third_kernel(pieces, at_ref, *refs):
    piece_refs = refs[:pieces]
    (
        first_ref, gate_ref, gain_ref, shift_ref, out_w_ref, out_bias_ref,
        out_ref, left_scr, x_scr,
    ) = refs[pieces:]
    rows, side, width = out_ref.shape
    hidden = gate_ref.shape[1]
    place = (at_ref[0] % PLANE) * rows
    near = PLANE * rows
    for s, piece in enumerate(piece_refs):
        left_scr[s] = piece[rows * side :, :].astype(F32)

    def columns(at):
        totals = [jnp.zeros((CHUNK, hidden), F32)] * rows
        for s, piece in enumerate(piece_refs):
            for a in range(rows):
                right = piece[pl.ds(a * side + at, CHUNK), :].astype(F32)
                for i in range(rows):
                    left = left_scr[s, pl.ds(a * near + place + i, 1), :]
                    totals[i] = totals[i] + left * right
        for i in range(rows):
            x_scr[i, pl.ds(at, CHUNK), :] = totals[i]

    if side == CHUNK:
        columns(0)
    else:
        pl.loop(0, side // CHUNK)(lambda n: columns(pl.multiple_of(n * CHUNK, CHUNK)))
    out_ref[...] = finish(
        first_ref[...], x_scr[...].reshape(rows * side, hidden), gate_ref[...],
        gain_ref, shift_ref, out_w_ref, out_bias_ref, 1,
    ).reshape(rows, side, width)


def body(pair, residue_mask, norm_gain, norm_bias, edge_w, edge_bias, out_w, out_bias):
    rows, side, width = pair.shape
    hidden = out_w.shape[1]
    dap = lax.axis_size("dap")
    planes = dap // PLANE
    at = lax.axis_index("dap").reshape(1)
    mask = residue_mask.reshape(1, side)
    params = pltpu.CompilerParams(vmem_limit_bytes=48 * 1024 * 1024)
    count = rows * side
    shape = jax.ShapeDtypeStruct

    def swap(piece, bits):
        return lax.ppermute(piece, "dap", [(device, device ^ bits) for device in range(dap)])

    def gather(sends):
        pieces = [None] * dap
        pieces[0] = sends[0]
        pieces[2] = swap(sends[0], 2)
        for k in range(planes - 1, 0, -1):
            pieces[PLANE * k] = swap(sends[k], PLANE * k)
        for k in range(planes - 1, 0, -1):
            pieces[PLANE * k + 2] = swap(pieces[PLANE * k], 2)
        for s in range(0, dap, 2):
            pieces[s + 1] = swap(pieces[s], 1)
        return pieces

    right, left, gate = pl.pallas_call(
        first_kernel,
        in_specs=[SMEM] + [VMEM] * 6,
        out_specs=[VMEM] * 3,
        out_shape=[
            shape((count, hidden), BF16),
            shape((count, hidden), F32),
            shape((count, width), F32),
        ],
        compiler_params=params,
        name="project_first",
    )(at, pair, mask, norm_gain, norm_bias, edge_w, edge_bias)
    pieces = gather([right] * planes)

    *sends, gate, first = pl.pallas_call(
        functools.partial(second_kernel, dap),
        in_specs=[SMEM] + [VMEM] * (dap + 10),
        out_specs=[VMEM] * (planes + 2),
        out_shape=[shape((count + PLANE * rows * rows, hidden), BF16)] * planes
        + [shape((count, width), F32)] * 2,
        scratch_shapes=[pltpu.VMEM((rows, side, hidden), F32)] * 2,
        compiler_params=params,
        name="contract_outgoing",
    )(
        at, *pieces, left, gate, pair, mask, norm_gain, norm_bias,
        out_w, out_bias, edge_w, edge_bias,
    )
    pieces = gather(sends)

    return pl.pallas_call(
        functools.partial(third_kernel, dap),
        in_specs=[SMEM] + [VMEM] * (dap + 6),
        out_specs=VMEM,
        out_shape=shape((rows, side, width), F32),
        scratch_shapes=[
            pltpu.VMEM((dap, PLANE * rows * rows, hidden), F32),
            pltpu.VMEM((rows, side, hidden), F32),
        ],
        compiler_params=params,
        name="contract_incoming",
    )(at, *pieces, first, gate, norm_gain, norm_bias, out_w, out_bias)


def solution(mesh):
    in_specs = (P(("groups", "dap"), None, None), P("groups"), P(), P(), P(), P(), P(), P())
    out_specs = P(("groups", "dap"), None, None)
    return jax.shard_map(body, mesh=mesh, in_specs=in_specs, out_specs=out_specs, check_vma=False)
```

```python
import functools

import jax
import jax.numpy as jnp
from jax import lax
from jax.experimental import pallas as pl
from jax.experimental.pallas import tpu as pltpu
from jax.sharding import PartitionSpec as P

F32 = jnp.float32
BF16 = jnp.bfloat16
VMEM = pl.BlockSpec(memory_space=pltpu.VMEM)
SMEM = pl.BlockSpec(memory_space=pltpu.SMEM)
PLANE = 4
CHUNK = 64
BLOCK = 256
PARAMS = pltpu.CompilerParams(vmem_limit_bytes=48 * 1024 * 1024)


def normalize(values, gain, shift):
    mean = jnp.mean(values, axis=-1, keepdims=True)
    centered = values - mean
    spread = jnp.mean(centered * centered, axis=-1, keepdims=True)
    return centered * lax.rsqrt(spread + 1e-05) * gain + shift


def sigmoid(values):
    return 0.5 * jnp.tanh(0.5 * values) + 0.5


def gated(normed, edge_w_ref, edge_bias_ref, layer, index, hidden):
    span = slice(index * hidden, (index + 2) * hidden)
    both = jnp.dot(normed, edge_w_ref[layer, :, span], preferred_element_type=F32)
    both = both + edge_bias_ref[layer : layer + 1, span]
    return sigmoid(both[:, :hidden]) * both[:, hidden:]


def masked(values, row, column, mask_ref):
    valid = jnp.sum(mask_ref[...].astype(F32), axis=1, keepdims=True)
    return jnp.where(jnp.maximum(row, column).astype(F32) < valid, values, 0.0)


def edges(normed_ref, out_ref, first_row, side, mask_ref, edge_w_ref, edge_bias_ref, layer, index):
    count, hidden = normed_ref.shape[0], out_ref.shape[1]
    size = min(count, BLOCK)

    def block(at):
        values = gated(
            normed_ref[pl.ds(at, size), :], edge_w_ref, edge_bias_ref, layer, index, hidden
        )
        position = at + lax.broadcasted_iota(jnp.int32, values.shape, 0)
        values = masked(values, first_row + position // side, position % side, mask_ref)
        out_ref[pl.ds(at, size), :] = values.astype(BF16).astype(out_ref.dtype)

    if count == size:
        block(0)
    else:
        pl.loop(0, count // size)(lambda n: block(pl.multiple_of(n * size, size)))


def gate_of(normed_ref, gate_ref, edge_w_ref, edge_bias_ref, layer):
    width = gate_ref.shape[1]
    low = edge_bias_ref.shape[1] - width
    value = jnp.dot(normed_ref[...], edge_w_ref[layer, :, low:], preferred_element_type=F32)
    gate_ref[...] = sigmoid(value + edge_bias_ref[layer : layer + 1, low:])


def finish(block, contracted, gate, gain_ref, shift_ref, out_w_ref, out_bias_ref, layer):
    normed = normalize(contracted, gain_ref[layer, 1:2, :], shift_ref[layer, 1:2, :]).astype(BF16)
    result = jnp.dot(normed, out_w_ref[layer], preferred_element_type=F32)
    return block + gate * (result + out_bias_ref[layer : layer + 1, :])


def norm_kernel(pair_ref, gain_ref, shift_ref, normed_ref):
    block = pair_ref[...].reshape(normed_ref.shape)
    normed_ref[...] = normalize(block, gain_ref[0, 0:1, :], shift_ref[0, 0:1, :]).astype(BF16)


def merge(low, a, b, shift):
    return jnp.where(low, a, b) + pltpu.roll(jnp.where(low, b, a), shift, 0)


def fold(parts, sub):
    low = (sub & 1) == 0
    first, second = merge(low, parts[0], parts[1], 1), merge(low, parts[2], parts[3], 1)
    return merge((sub & 2) == 0, first, second, 2)


def row_sums(left_ref, piece_ref, a, rows, side):
    hidden = left_ref.shape[1]

    def chunk(at, totals):
        right = piece_ref[pl.ds(a * side + at, CHUNK), :].astype(F32)
        sums = []
        for i in range(rows):
            product = left_ref[pl.ds(i * side + at, CHUNK), :] * right
            sums.append(jnp.sum(product.reshape(CHUNK // 8, 8, hidden), axis=0))
        return [t + s for t, s in zip(totals, sums)] if totals else sums

    totals = chunk(0, None)
    if side > CHUNK:
        totals = lax.fori_loop(
            1, side // CHUNK, lambda n, t: chunk(pl.multiple_of(n * CHUNK, CHUNK), t), totals
        )
    return totals


def piece_products(left_ref, piece_ref, rows, side):
    sub = lax.broadcasted_iota(jnp.int32, (8, left_ref.shape[1]), 0)
    totals = [row_sums(left_ref, piece_ref, a, rows, side) for a in range(rows)]
    return [fold([totals[a][i] for a in range(rows)], sub) for i in range(rows)]


def outgoing_edges_kernel(held, rows, at_ref, *refs):
    normed, refs = refs[: len(held)], refs[len(held) :]
    mask_ref, edge_w_ref, edge_bias_ref, *refs = refs
    own = held[0] == 0
    if own:
        right_ref, part_ref, left_ref, gate_ref = refs
    else:
        left_ref, right_ref, part_ref = refs
    side = left_ref.shape[0] // rows
    shared = (side, mask_ref, edge_w_ref, edge_bias_ref, 0)
    if own:
        edges(normed[0], left_ref, at_ref[0] * rows, *shared, 0)
        gate_of(normed[0], gate_ref, edge_w_ref, edge_bias_ref, 0)
    for n, s in enumerate(held):
        edges(normed[n], right_ref.at[n], (at_ref[0] ^ s) * rows, *shared, 2)
        for i, part in enumerate(piece_products(left_ref, right_ref.at[n], rows, side)):
            part_ref[n, i] = part


def outgoing_kernel(left_ref, piece_ref, part_ref):
    rows = part_ref.shape[1]
    side = left_ref.shape[0] // rows
    for n in range(piece_ref.shape[0]):
        for i, part in enumerate(piece_products(left_ref, piece_ref.at[n], rows, side)):
            part_ref[n, i] = part


def outgoing_finish_kernel(last, given, at_ref, piece_ref, *refs):
    parts, refs = refs[: len(given)], refs[len(given) :]
    (
        left_ref, gate_ref, pair_ref, gain_ref, shift_ref, out_w_ref, out_bias_ref,
        first_ref, normed_ref, x_scr,
    ) = refs
    rows, side, width = pair_ref.shape
    hidden = left_ref.shape[1]
    sub = lax.broadcasted_iota(jnp.int32, (8, hidden), 0)
    me = at_ref[0]
    low = (sub & 4) == 0
    known = {s: (ref, n) for ref, held in zip(parts, given) for n, s in enumerate(held)}

    def part_of(s):
        if s in last:
            return piece_products(left_ref, piece_ref.at[last.index(s)], rows, side)
        ref, n = known[s]
        return [ref[n, i] for i in range(rows)]

    for s in range(0, len(known) + len(last), 2):
        at = pl.multiple_of((me >> 1 ^ s >> 1) * 2 * rows, 2 * rows)
        for i, (a, b) in enumerate(zip(part_of(s), part_of(s + 1))):
            x = merge(low, a, b, 4)
            x = jnp.where(me & 1 == 0, x, pltpu.roll(x, rows, 0))
            x_scr[i, pl.ds(at, 2 * rows), :] = x

    block = pair_ref[...].reshape(rows * side, width)
    contracted = x_scr[...].reshape(rows * side, hidden)
    first = finish(
        block, contracted, gate_ref[...], gain_ref, shift_ref, out_w_ref, out_bias_ref, 0
    )
    first_ref[...] = first
    normed_ref[...] = normalize(first, gain_ref[1, 0:1, :], shift_ref[1, 0:1, :]).astype(BF16)


def add_pieces(pieces, left_scr, x_ref, start):
    rows, side, hidden = x_ref.shape
    for n, (piece, came) in enumerate(pieces):
        left_scr[n] = piece[rows * side :, :].astype(F32)

    def columns(at):
        totals = [start(i, at) for i in range(rows)]
        for n, (piece, came) in enumerate(pieces):
            for a in range(rows):
                right = piece[pl.ds(a * side + at, CHUNK), :].astype(F32)
                for i in range(rows):
                    row = a * 2 * rows + came * rows + i
                    totals[i] = totals[i] + left_scr[n, row : row + 1, :] * right
        for i in range(rows):
            x_ref[i, pl.ds(at, CHUNK), :] = totals[i]

    if side == CHUNK:
        columns(0)
    else:
        pl.loop(0, side // CHUNK)(lambda n: columns(pl.multiple_of(n * CHUNK, CHUNK)))


def incoming_edges_kernel(held, at_ref, *refs):
    normed, refs = refs[: len(held)], refs[len(held) :]
    mask_ref, edge_w_ref, edge_bias_ref, *refs = refs
    if held[0] == 0:
        out_ref, x_ref, gate_ref, left_scr = refs
        gate_of(normed[0], gate_ref, edge_w_ref, edge_bias_ref, 1)
    else:
        before_ref, out_ref, x_ref, left_scr = refs
    rows, side, hidden = x_ref.shape
    me = at_ref[0]
    chip = me >> 1
    columns, places = [], []
    for n, s in enumerate(held):
        edges(
            normed[n], out_ref.at[n, pl.ds(0, rows * side)], (me ^ s) * rows, side,
            mask_ref, edge_w_ref, edge_bias_ref, 1, 2,
        )
        for a in range(rows):
            both = normed[n][pl.ds(pl.multiple_of(a * side + (chip >> 1) * 16, 16), 16), :]
            both = both.astype(F32)
            columns.append(jnp.where(chip & 1 == 0, both[:8], both[8:]))
            places.append(jnp.full((8, hidden), (me ^ s) * rows + a, jnp.int32))
    left = gated(
        jnp.concatenate(columns, 0).astype(BF16), edge_w_ref, edge_bias_ref, 1, 0, hidden
    )
    column = chip * 8 + lax.broadcasted_iota(jnp.int32, left.shape, 0) % 8
    left = masked(left, jnp.concatenate(places, 0), column, mask_ref)
    left = left.reshape(len(held) * rows, 8, hidden)
    left = jnp.where(me & 1 == 0, left, pltpu.roll(left, rows, 1))
    left = left.reshape(len(held), rows * 8, hidden).astype(BF16)
    for n in range(len(held)):
        out_ref[n, rows * side :, :] = left[n]

    def start(i, at):
        if held[0] == 0:
            return jnp.zeros((CHUNK, hidden), F32)
        return before_ref[i, pl.ds(at, CHUNK), :]

    add_pieces([(out_ref.at[n], 0) for n in range(len(held))], left_scr, x_ref, start)


def incoming_kernel(before_ref, piece_ref, x_ref, left_scr):
    pieces = [(piece_ref.at[n], 1) for n in range(piece_ref.shape[0])]
    add_pieces(pieces, left_scr, x_ref, lambda i, at: before_ref[i, pl.ds(at, CHUNK), :])


def incoming_finish_kernel(
    before_ref, piece_ref, first_ref, gate_ref, gain_ref, shift_ref, out_w_ref, out_bias_ref,
    out_ref, left_scr, x_scr,
):
    rows, side, width = out_ref.shape
    hidden = gate_ref.shape[1]
    pieces = [(piece_ref.at[n], 1) for n in range(piece_ref.shape[0])]
    add_pieces(pieces, left_scr, x_scr, lambda i, at: before_ref[i, pl.ds(at, CHUNK), :])
    out_ref[...] = finish(
        first_ref[...], x_scr[...].reshape(rows * side, hidden), gate_ref[...],
        gain_ref, shift_ref, out_w_ref, out_bias_ref, 1,
    ).reshape(rows, side, width)


def call(kernel, name, outs, *operands, scalar=None, scratch=(), flops=0):
    given = operands if scalar is None else (scalar, *operands)
    cost = pl.CostEstimate(flops=flops, bytes_accessed=flops // 64, transcendentals=0)
    return pl.pallas_call(
        kernel,
        in_specs=[SMEM] * (scalar is not None) + [VMEM] * len(operands),
        out_specs=[VMEM] * len(outs),
        out_shape=[jax.ShapeDtypeStruct(*out) for out in outs],
        scratch_shapes=[pltpu.VMEM(*one) for one in scratch],
        compiler_params=PARAMS,
        cost_estimate=cost if flops else None,
        name=name,
    )(*given)


def body(pair, residue_mask, norm_gain, norm_bias, edge_w, edge_bias, out_w, out_bias):
    rows, side, width = pair.shape
    hidden = out_w.shape[1]
    dap = lax.axis_size("dap")
    planes = dap // PLANE
    me = lax.axis_index("dap").reshape(1)
    mask = residue_mask.reshape(1, side)
    norms = (norm_gain, norm_bias)
    weights = (mask, edge_w, edge_bias)
    count = rows * side
    span = count + 2 * rows * rows

    def swap(piece, bits):
        return lax.ppermute(piece, "dap", [(device, device ^ bits) for device in range(dap)])

    def gather(own):
        pieces = {0: own, 2: swap(own, 2)}
        for k in range(planes - 1, 0, -1):
            pieces[PLANE * k] = swap(own, PLANE * k)
        for k in range(planes - 1, 0, -1):
            pieces[PLANE * k + 2] = swap(pieces[PLANE * k], 2)
        return pieces

    groups = (
        [PLANE * k for k in range(planes)],
        [2] + [PLANE * k + 2 for k in range(planes - 1, 0, -1)],
    )
    came = [[s ^ 1 for s in group] for group in groups]

    def work(pieces):
        return 2 * pieces * count * rows * hidden

    (normed,) = call(norm_kernel, "norm", [((count, width), BF16)], pair, *norms)
    pieces = gather(normed)
    others, parts = [], []
    for group in groups:
        held = len(group)
        outs = [((held, count, hidden), BF16), ((held, rows, 8, hidden), F32)]
        if group[0] == 0:
            outs += [((count, hidden), F32), ((count, width), F32)]
        right, part, *rest = call(
            functools.partial(outgoing_edges_kernel, group, rows),
            "outgoing_edges", outs, *[pieces[s] for s in group], *weights,
            *([left] if group[0] else []), scalar=me, flops=work(held),
        )
        if rest:
            left, gate = rest
        parts.append(part)
        others.append(swap(right, 1))
    known = [*groups, came[0]]
    (part,) = call(
        outgoing_kernel, "outgoing", [((planes, rows, 8, hidden), F32)],
        left, others[0], flops=work(planes),
    )
    first, normed = call(
        functools.partial(outgoing_finish_kernel, came[1], known), "outgoing_finish",
        [((count, width), F32), ((count, width), BF16)],
        others[1], *parts, part, left, gate, pair, *norms, out_w, out_bias,
        scalar=me, scratch=[((rows, side, hidden), F32)],
    )

    pieces = gather(normed)
    others, x = [], []
    for group in groups:
        held = len(group)
        outs = [((held, span, hidden), BF16), ((rows, side, hidden), F32)]
        if group[0] == 0:
            outs += [((count, width), F32)]
        edge, *x = call(
            functools.partial(incoming_edges_kernel, group),
            "incoming_edges", outs, *[pieces[s] for s in group], *weights, *x,
            scalar=me, scratch=[((held, 2 * rows * rows, hidden), F32)], flops=work(held),
        )
        if group[0] == 0:
            gate = x.pop()
        others.append(swap(edge, 1))
    x = call(
        incoming_kernel, "incoming", [((rows, side, hidden), F32)], *x, others[0],
        scratch=[((planes, 2 * rows * rows, hidden), F32)], flops=work(planes),
    )
    (out,) = call(
        incoming_finish_kernel, "incoming_finish", [(pair.shape, F32)],
        *x, others[1], first, gate, *norms, out_w, out_bias,
        scratch=[((planes, 2 * rows * rows, hidden), F32), ((rows, side, hidden), F32)],
    )
    return out


def solution(mesh):
    in_specs = (P(("groups", "dap"), None, None), P("groups"), P(), P(), P(), P(), P(), P())
    out_specs = P(("groups", "dap"), None, None)
    return jax.shard_map(body, mesh=mesh, in_specs=in_specs, out_specs=out_specs, check_vma=False)
```

```python
import functools

import jax
import jax.numpy as jnp
from jax import lax
from jax.experimental import pallas as pl
from jax.experimental.pallas import tpu as pltpu
from jax.sharding import PartitionSpec as P

F32 = jnp.float32
BF16 = jnp.bfloat16
VMEM = pl.BlockSpec(memory_space=pltpu.VMEM)
SMEM = pl.BlockSpec(memory_space=pltpu.SMEM)
PLANE = 4
CHUNK = 64
BLOCK = 256
PARAMS = pltpu.CompilerParams(vmem_limit_bytes=48 * 1024 * 1024)


def normalize(values, gain, shift):
    mean = jnp.mean(values, axis=-1, keepdims=True)
    centered = values - mean
    spread = jnp.mean(centered * centered, axis=-1, keepdims=True)
    return centered * lax.rsqrt(spread + 1e-05) * gain + shift


def sigmoid(values):
    return 0.5 * jnp.tanh(0.5 * values) + 0.5


def gated(normed, edge_w_ref, edge_bias_ref, layer, index, hidden):
    span = slice(index * hidden, (index + 2) * hidden)
    both = jnp.dot(normed, edge_w_ref[layer, :, span], preferred_element_type=F32)
    both = both + edge_bias_ref[layer : layer + 1, span]
    return sigmoid(both[:, :hidden]) * both[:, hidden:]


def masked(values, row, column, mask_ref):
    valid = jnp.sum(mask_ref[...].astype(F32), axis=1, keepdims=True)
    return jnp.where(jnp.maximum(row, column).astype(F32) < valid, values, 0.0)


def edges(normed_ref, out_ref, first_row, side, mask_ref, edge_w_ref, edge_bias_ref, layer, index):
    count, hidden = normed_ref.shape[0], out_ref.shape[1]
    size = min(count, BLOCK)

    def block(at):
        values = gated(
            normed_ref[pl.ds(at, size), :], edge_w_ref, edge_bias_ref, layer, index, hidden
        )
        position = at + lax.broadcasted_iota(jnp.int32, values.shape, 0)
        values = masked(values, first_row + position // side, position % side, mask_ref)
        out_ref[pl.ds(at, size), :] = values.astype(BF16).astype(out_ref.dtype)

    if count == size:
        block(0)
    else:
        pl.loop(0, count // size)(lambda n: block(pl.multiple_of(n * size, size)))


def gate_of(normed_ref, gate_ref, edge_w_ref, edge_bias_ref, layer):
    width = gate_ref.shape[1]
    low = edge_bias_ref.shape[1] - width
    value = jnp.dot(normed_ref[...], edge_w_ref[layer, :, low:], preferred_element_type=F32)
    gate_ref[...] = sigmoid(value + edge_bias_ref[layer : layer + 1, low:])


def finish(block, contracted, gate, gain_ref, shift_ref, out_w_ref, out_bias_ref, layer):
    normed = normalize(contracted, gain_ref[layer, 1:2, :], shift_ref[layer, 1:2, :]).astype(BF16)
    result = jnp.dot(normed, out_w_ref[layer], preferred_element_type=F32)
    return block + gate * (result + out_bias_ref[layer : layer + 1, :])


def norm_kernel(*refs):
    count = len(refs) // 2 - 1
    given, kept, (normed_ref, sems) = refs[:count], refs[count : 2 * count], refs[2 * count :]
    copies = [
        pltpu.make_async_copy(source, target, sems.at[n])
        for n, (source, target) in enumerate(zip(given, kept))
    ]
    for copy in copies:
        copy.start()
    for copy in copies[:3]:
        copy.wait()
    pair_ref, gain_ref, shift_ref = kept[:3]
    block = pair_ref[...].reshape(normed_ref.shape)
    normed_ref[...] = normalize(block, gain_ref[0, 0:1, :], shift_ref[0, 0:1, :]).astype(BF16)
    for copy in copies[3:]:
        copy.wait()


def merge(low, a, b, shift):
    return jnp.where(low, a, b) + pltpu.roll(jnp.where(low, b, a), shift, 0)


def fold(parts, sub):
    low = (sub & 1) == 0
    first, second = merge(low, parts[0], parts[1], 1), merge(low, parts[2], parts[3], 1)
    return merge((sub & 2) == 0, first, second, 2)


def row_sums(left_ref, piece_ref, a, rows, side):
    hidden = left_ref.shape[1]

    def chunk(at, totals):
        right = piece_ref[pl.ds(a * side + at, CHUNK), :].astype(F32)
        sums = []
        for i in range(rows):
            product = left_ref[pl.ds(i * side + at, CHUNK), :] * right
            sums.append(jnp.sum(product.reshape(CHUNK // 8, 8, hidden), axis=0))
        return [t + s for t, s in zip(totals, sums)] if totals else sums

    totals = chunk(0, None)
    if side > CHUNK:
        totals = lax.fori_loop(
            1, side // CHUNK, lambda n, t: chunk(pl.multiple_of(n * CHUNK, CHUNK), t), totals
        )
    return totals


def piece_products(left_ref, piece_ref, rows, side):
    sub = lax.broadcasted_iota(jnp.int32, (8, left_ref.shape[1]), 0)
    totals = [row_sums(left_ref, piece_ref, a, rows, side) for a in range(rows)]
    return [fold([totals[a][i] for a in range(rows)], sub) for i in range(rows)]


def outgoing_edges_kernel(held, rows, at_ref, *refs):
    normed, refs = refs[: len(held)], refs[len(held) :]
    mask_ref, edge_w_ref, edge_bias_ref, *refs = refs
    own = held[0] == 0
    if own:
        right_ref, part_ref, left_ref, gate_ref = refs
    else:
        left_ref, right_ref, part_ref = refs
    side = left_ref.shape[0] // rows
    shared = (side, mask_ref, edge_w_ref, edge_bias_ref, 0)
    if own:
        edges(normed[0], left_ref, at_ref[0] * rows, *shared, 0)
        gate_of(normed[0], gate_ref, edge_w_ref, edge_bias_ref, 0)
    for n, s in enumerate(held):
        edges(normed[n], right_ref.at[n], (at_ref[0] ^ s) * rows, *shared, 2)
        for i, part in enumerate(piece_products(left_ref, right_ref.at[n], rows, side)):
            part_ref[n, i] = part


def outgoing_kernel(left_ref, piece_ref, part_ref):
    rows = part_ref.shape[1]
    side = left_ref.shape[0] // rows
    for n in range(piece_ref.shape[0]):
        for i, part in enumerate(piece_products(left_ref, piece_ref.at[n], rows, side)):
            part_ref[n, i] = part


def outgoing_finish_kernel(last, given, at_ref, piece_ref, *refs):
    parts, refs = refs[: len(given)], refs[len(given) :]
    (
        left_ref, gate_ref, pair_ref, gain_ref, shift_ref, out_w_ref, out_bias_ref,
        first_ref, normed_ref, x_scr,
    ) = refs
    rows, side, width = pair_ref.shape
    hidden = left_ref.shape[1]
    sub = lax.broadcasted_iota(jnp.int32, (8, hidden), 0)
    me = at_ref[0]
    low = (sub & 4) == 0
    known = {s: (ref, n) for ref, held in zip(parts, given) for n, s in enumerate(held)}

    def part_of(s):
        if s in last:
            return piece_products(left_ref, piece_ref.at[last.index(s)], rows, side)
        ref, n = known[s]
        return [ref[n, i] for i in range(rows)]

    for s in range(0, len(known) + len(last), 2):
        at = pl.multiple_of((me >> 1 ^ s >> 1) * 2 * rows, 2 * rows)
        for i, (a, b) in enumerate(zip(part_of(s), part_of(s + 1))):
            x = merge(low, a, b, 4)
            x = jnp.where(me & 1 == 0, x, pltpu.roll(x, rows, 0))
            x_scr[i, pl.ds(at, 2 * rows), :] = x

    block = pair_ref[...].reshape(rows * side, width)
    contracted = x_scr[...].reshape(rows * side, hidden)
    first = finish(
        block, contracted, gate_ref[...], gain_ref, shift_ref, out_w_ref, out_bias_ref, 0
    )
    first_ref[...] = first
    normed_ref[...] = normalize(first, gain_ref[1, 0:1, :], shift_ref[1, 0:1, :]).astype(BF16)


def add_pieces(pieces, left_scr, x_ref, start):
    rows, side, hidden = x_ref.shape
    for n, (piece, came) in enumerate(pieces):
        left_scr[n] = piece[rows * side :, :].astype(F32)

    def columns(at):
        totals = [start(i, at) for i in range(rows)]
        for n, (piece, came) in enumerate(pieces):
            for a in range(rows):
                right = piece[pl.ds(a * side + at, CHUNK), :].astype(F32)
                for i in range(rows):
                    row = a * 2 * rows + came * rows + i
                    totals[i] = totals[i] + left_scr[n, row : row + 1, :] * right
        for i in range(rows):
            x_ref[i, pl.ds(at, CHUNK), :] = totals[i]

    if side == CHUNK:
        columns(0)
    else:
        pl.loop(0, side // CHUNK)(lambda n: columns(pl.multiple_of(n * CHUNK, CHUNK)))


def incoming_edges_kernel(held, at_ref, *refs):
    normed, refs = refs[: len(held)], refs[len(held) :]
    mask_ref, edge_w_ref, edge_bias_ref, *refs = refs
    if held[0] == 0:
        out_ref, x_ref, gate_ref, left_scr = refs
        gate_of(normed[0], gate_ref, edge_w_ref, edge_bias_ref, 1)
    else:
        before_ref, out_ref, x_ref, left_scr = refs
    rows, side, hidden = x_ref.shape
    me = at_ref[0]
    chip = me >> 1
    columns, places = [], []
    for n, s in enumerate(held):
        edges(
            normed[n], out_ref.at[n, pl.ds(0, rows * side)], (me ^ s) * rows, side,
            mask_ref, edge_w_ref, edge_bias_ref, 1, 2,
        )
        for a in range(rows):
            both = normed[n][pl.ds(pl.multiple_of(a * side + (chip >> 1) * 16, 16), 16), :]
            both = both.astype(F32)
            columns.append(jnp.where(chip & 1 == 0, both[:8], both[8:]))
            places.append(jnp.full((8, hidden), (me ^ s) * rows + a, jnp.int32))
    left = gated(
        jnp.concatenate(columns, 0).astype(BF16), edge_w_ref, edge_bias_ref, 1, 0, hidden
    )
    column = chip * 8 + lax.broadcasted_iota(jnp.int32, left.shape, 0) % 8
    left = masked(left, jnp.concatenate(places, 0), column, mask_ref)
    left = left.reshape(len(held) * rows, 8, hidden)
    left = jnp.where(me & 1 == 0, left, pltpu.roll(left, rows, 1))
    left = left.reshape(len(held), rows * 8, hidden).astype(BF16)
    for n in range(len(held)):
        out_ref[n, rows * side :, :] = left[n]

    def start(i, at):
        if held[0] == 0:
            return jnp.zeros((CHUNK, hidden), F32)
        return before_ref[i, pl.ds(at, CHUNK), :]

    add_pieces([(out_ref.at[n], 0) for n in range(len(held))], left_scr, x_ref, start)


def incoming_kernel(before_ref, piece_ref, x_ref, left_scr):
    pieces = [(piece_ref.at[n], 1) for n in range(piece_ref.shape[0])]
    add_pieces(pieces, left_scr, x_ref, lambda i, at: before_ref[i, pl.ds(at, CHUNK), :])


def incoming_finish_kernel(
    before_ref, piece_ref, first_ref, gate_ref, gain_ref, shift_ref, out_w_ref, out_bias_ref,
    out_ref, left_scr, x_scr,
):
    rows, side, width = out_ref.shape
    hidden = gate_ref.shape[1]
    pieces = [(piece_ref.at[n], 1) for n in range(piece_ref.shape[0])]
    add_pieces(pieces, left_scr, x_scr, lambda i, at: before_ref[i, pl.ds(at, CHUNK), :])
    out_ref[...] = finish(
        first_ref[...], x_scr[...].reshape(rows * side, hidden), gate_ref[...],
        gain_ref, shift_ref, out_w_ref, out_bias_ref, 1,
    ).reshape(rows, side, width)


def call(kernel, name, outs, *operands, scalar=None, scratch=(), flops=0):
    given = operands if scalar is None else (scalar, *operands)
    cost = pl.CostEstimate(flops=flops, bytes_accessed=flops // 64, transcendentals=0)
    return pl.pallas_call(
        kernel,
        in_specs=[SMEM] * (scalar is not None) + [VMEM] * len(operands),
        out_specs=[VMEM] * len(outs),
        out_shape=[jax.ShapeDtypeStruct(*out) for out in outs],
        scratch_shapes=[pltpu.VMEM(*one) for one in scratch],
        compiler_params=PARAMS,
        cost_estimate=cost if flops else None,
        name=name,
    )(*given)


def body(pair, residue_mask, norm_gain, norm_bias, edge_w, edge_bias, out_w, out_bias):
    rows, side, width = pair.shape
    hidden = out_w.shape[1]
    dap = lax.axis_size("dap")
    planes = dap // PLANE
    me = lax.axis_index("dap").reshape(1)
    mask = residue_mask.reshape(1, side)
    count = rows * side
    arguments = (pair, norm_gain, norm_bias, mask, edge_w, edge_bias, out_w, out_bias)
    *kept, normed = pl.pallas_call(
        norm_kernel,
        in_specs=[pl.BlockSpec(memory_space=pltpu.HBM)] * len(arguments),
        out_specs=[VMEM] * (len(arguments) + 1),
        out_shape=[jax.ShapeDtypeStruct(value.shape, value.dtype) for value in arguments]
        + [jax.ShapeDtypeStruct((count, width), BF16)],
        scratch_shapes=[pltpu.SemaphoreType.DMA((len(arguments),))],
        compiler_params=PARAMS,
        name="norm",
    )(*[pltpu.with_memory_space_constraint(value, pltpu.HBM) for value in arguments])
    pair, norm_gain, norm_bias, mask, edge_w, edge_bias, out_w, out_bias = kept
    norms = (norm_gain, norm_bias)
    weights = (mask, edge_w, edge_bias)
    span = count + 2 * rows * rows

    def swap(piece, bits):
        return lax.ppermute(piece, "dap", [(device, device ^ bits) for device in range(dap)])

    def gather(own):
        pieces = {0: own, 2: swap(own, 2)}
        for k in range(planes - 1, 0, -1):
            pieces[PLANE * k] = swap(own, PLANE * k)
        for k in range(planes - 1, 0, -1):
            pieces[PLANE * k + 2] = swap(pieces[PLANE * k], 2)
        return pieces

    groups = (
        [PLANE * k for k in range(planes)],
        [2] + [PLANE * k + 2 for k in range(planes - 1, 0, -1)],
    )
    came = [[s ^ 1 for s in group] for group in groups]

    def work(pieces):
        return 2 * pieces * count * rows * hidden

    pieces = gather(normed)
    others, parts = [], []
    for group in groups:
        held = len(group)
        outs = [((held, count, hidden), BF16), ((held, rows, 8, hidden), F32)]
        if group[0] == 0:
            outs += [((count, hidden), F32), ((count, width), F32)]
        right, part, *rest = call(
            functools.partial(outgoing_edges_kernel, group, rows),
            "outgoing_edges", outs, *[pieces[s] for s in group], *weights,
            *([left] if group[0] else []), scalar=me, flops=work(held),
        )
        if rest:
            left, gate = rest
        parts.append(part)
        others.append(swap(right, 1))
    known = [*groups, came[0]]
    (part,) = call(
        outgoing_kernel, "outgoing", [((planes, rows, 8, hidden), F32)],
        left, others[0], flops=work(planes),
    )
    first, normed = call(
        functools.partial(outgoing_finish_kernel, came[1], known), "outgoing_finish",
        [((count, width), F32), ((count, width), BF16)],
        others[1], *parts, part, left, gate, pair, *norms, out_w, out_bias,
        scalar=me, scratch=[((rows, side, hidden), F32)],
    )

    pieces = gather(normed)
    others, x = [], []
    for group in groups:
        held = len(group)
        outs = [((held, span, hidden), BF16), ((rows, side, hidden), F32)]
        if group[0] == 0:
            outs += [((count, width), F32)]
        edge, *x = call(
            functools.partial(incoming_edges_kernel, group),
            "incoming_edges", outs, *[pieces[s] for s in group], *weights, *x,
            scalar=me, scratch=[((held, 2 * rows * rows, hidden), F32)], flops=work(held),
        )
        if group[0] == 0:
            gate = x.pop()
        others.append(swap(edge, 1))
    x = call(
        incoming_kernel, "incoming", [((rows, side, hidden), F32)], *x, others[0],
        scratch=[((planes, 2 * rows * rows, hidden), F32)], flops=work(planes),
    )
    (out,) = call(
        incoming_finish_kernel, "incoming_finish", [(pair.shape, F32)],
        *x, others[1], first, gate, *norms, out_w, out_bias,
        scratch=[((planes, 2 * rows * rows, hidden), F32), ((rows, side, hidden), F32)],
    )
    return out


def solution(mesh):
    in_specs = (P(("groups", "dap"), None, None), P("groups"), P(), P(), P(), P(), P(), P())
    out_specs = P(("groups", "dap"), None, None)
    return jax.shard_map(body, mesh=mesh, in_specs=in_specs, out_specs=out_specs, check_vma=False)
```

```python
import functools

import jax
import jax.numpy as jnp
from jax import lax
from jax.experimental import pallas as pl
from jax.experimental.pallas import tpu as pltpu
from jax.sharding import PartitionSpec as P

F32 = jnp.float32
BF16 = jnp.bfloat16
VMEM = pl.BlockSpec(memory_space=pltpu.VMEM)
SMEM = pl.BlockSpec(memory_space=pltpu.SMEM)
PLANE = 4
CHUNK = 64
BLOCK = 256
PARAMS = pltpu.CompilerParams(vmem_limit_bytes=48 * 1024 * 1024)


def normalize(values, gain, shift):
    mean = jnp.mean(values, axis=-1, keepdims=True)
    centered = values - mean
    spread = jnp.mean(centered * centered, axis=-1, keepdims=True)
    return centered * lax.rsqrt(spread + 1e-05) * gain + shift


def sigmoid(values):
    return 0.5 * jnp.tanh(0.5 * values) + 0.5


def gated(normed, edge_w_ref, edge_bias_ref, layer, index, hidden):
    span = slice(index * hidden, (index + 2) * hidden)
    both = jnp.dot(normed, edge_w_ref[layer, :, span], preferred_element_type=F32)
    both = both + edge_bias_ref[layer : layer + 1, span]
    return sigmoid(both[:, :hidden]) * both[:, hidden:]


def masked(values, row, column, mask_ref):
    valid = jnp.sum(mask_ref[...].astype(F32), axis=1, keepdims=True)
    return jnp.where(jnp.maximum(row, column).astype(F32) < valid, values, 0.0)


def edges(normed_ref, out_ref, first_row, side, mask_ref, edge_w_ref, edge_bias_ref, layer, index):
    count, hidden = normed_ref.shape[0], out_ref.shape[1]
    size = min(count, BLOCK)

    def block(at):
        values = gated(
            normed_ref[pl.ds(at, size), :], edge_w_ref, edge_bias_ref, layer, index, hidden
        )
        position = at + lax.broadcasted_iota(jnp.int32, values.shape, 0)
        values = masked(values, first_row + position // side, position % side, mask_ref)
        out_ref[pl.ds(at, size), :] = values.astype(BF16).astype(out_ref.dtype)

    if count == size:
        block(0)
    else:
        pl.loop(0, count // size)(lambda n: block(pl.multiple_of(n * size, size)))


def gate_of(normed_ref, gate_ref, edge_w_ref, edge_bias_ref, layer):
    width = gate_ref.shape[1]
    low = edge_bias_ref.shape[1] - width
    value = jnp.dot(normed_ref[...], edge_w_ref[layer, :, low:], preferred_element_type=F32)
    gate_ref[...] = sigmoid(value + edge_bias_ref[layer : layer + 1, low:])


def finish(block, contracted, gate, gain_ref, shift_ref, out_w_ref, out_bias_ref, layer):
    normed = normalize(contracted, gain_ref[layer, 1:2, :], shift_ref[layer, 1:2, :]).astype(BF16)
    result = jnp.dot(normed, out_w_ref[layer], preferred_element_type=F32)
    return block + gate * (result + out_bias_ref[layer : layer + 1, :])


def norm_kernel(*refs):
    count = len(refs) // 2 - 1
    given, kept, (normed_ref, sems) = refs[:count], refs[count : 2 * count], refs[2 * count :]
    copies = [
        pltpu.make_async_copy(source, target, sems.at[n])
        for n, (source, target) in enumerate(zip(given, kept))
    ]
    for copy in copies:
        copy.start()
    for copy in copies[:3]:
        copy.wait()
    pair_ref, gain_ref, shift_ref = kept[:3]
    block = pair_ref[...].reshape(normed_ref.shape)
    normed_ref[...] = normalize(block, gain_ref[0, 0:1, :], shift_ref[0, 0:1, :]).astype(BF16)
    for copy in copies[3:]:
        copy.wait()


def merge(low, a, b, shift):
    return jnp.where(low, a, b) + pltpu.roll(jnp.where(low, b, a), shift, 0)


def fold(parts, sub):
    low = (sub & 1) == 0
    first, second = merge(low, parts[0], parts[1], 1), merge(low, parts[2], parts[3], 1)
    return merge((sub & 2) == 0, first, second, 2)


def row_sums(left_ref, piece_ref, a, rows, side):
    hidden = left_ref.shape[1]

    def chunk(at, totals):
        right = piece_ref[pl.ds(a * side + at, CHUNK), :].astype(F32)
        sums = []
        for i in range(rows):
            product = left_ref[pl.ds(i * side + at, CHUNK), :] * right
            sums.append(jnp.sum(product.reshape(CHUNK // 8, 8, hidden), axis=0))
        return [t + s for t, s in zip(totals, sums)] if totals else sums

    totals = chunk(0, None)
    if side > CHUNK:
        totals = lax.fori_loop(
            1, side // CHUNK, lambda n, t: chunk(pl.multiple_of(n * CHUNK, CHUNK), t), totals
        )
    return totals


def piece_products(left_ref, piece_ref, rows, side):
    sub = lax.broadcasted_iota(jnp.int32, (8, left_ref.shape[1]), 0)
    totals = [row_sums(left_ref, piece_ref, a, rows, side) for a in range(rows)]
    return [fold([totals[a][i] for a in range(rows)], sub) for i in range(rows)]


def outgoing_edges_kernel(held, rows, at_ref, *refs):
    normed, refs = refs[: len(held)], refs[len(held) :]
    mask_ref, edge_w_ref, edge_bias_ref, *refs = refs
    own = held[0] == 0
    if own:
        right_ref, part_ref, left_ref, gate_ref = refs
    else:
        left_ref, right_ref, part_ref = refs
    side = left_ref.shape[0] // rows
    shared = (side, mask_ref, edge_w_ref, edge_bias_ref, 0)
    if own:
        edges(normed[0], left_ref, at_ref[0] * rows, *shared, 0)
        gate_of(normed[0], gate_ref, edge_w_ref, edge_bias_ref, 0)
    for n, s in enumerate(held):
        edges(normed[n], right_ref.at[n], (at_ref[0] ^ s) * rows, *shared, 2)
        for i, part in enumerate(piece_products(left_ref, right_ref.at[n], rows, side)):
            part_ref[n, i] = part


def outgoing_last_kernel(last, rows, at_ref, normed_ref, mask_ref, edge_w_ref, edge_bias_ref, *refs):
    before_ref, right_ref = refs
    count = before_ref.shape[0]
    side = normed_ref.shape[0] // rows
    right_ref[:count] = before_ref[...]
    edges(
        normed_ref, right_ref.at[count], (at_ref[0] ^ last) * rows, side,
        mask_ref, edge_w_ref, edge_bias_ref, 0, 2,
    )


def outgoing_kernel(left_ref, piece_ref, last_ref, part_ref):
    rows = part_ref.shape[1]
    side = left_ref.shape[0] // rows
    count = piece_ref.shape[0]
    pieces = [piece_ref.at[n] for n in range(count)] + [last_ref.at[last_ref.shape[0] - 1]]
    for n, piece in enumerate(pieces):
        for i, part in enumerate(piece_products(left_ref, piece, rows, side)):
            part_ref[n, i] = part


def outgoing_finish_kernel(last, given, at_ref, piece_ref, *refs):
    parts, refs = refs[: len(given)], refs[len(given) :]
    (
        left_ref, gate_ref, pair_ref, gain_ref, shift_ref, out_w_ref, out_bias_ref,
        first_ref, normed_ref, x_scr,
    ) = refs
    rows, side, width = pair_ref.shape
    hidden = left_ref.shape[1]
    sub = lax.broadcasted_iota(jnp.int32, (8, hidden), 0)
    me = at_ref[0]
    low = (sub & 4) == 0
    known = {s: (ref, n) for ref, held in zip(parts, given) for n, s in enumerate(held)}

    def part_of(s):
        if s in last:
            return piece_products(left_ref, piece_ref.at[last.index(s)], rows, side)
        ref, n = known[s]
        return [ref[n, i] for i in range(rows)]

    for s in range(0, len(known) + len(last), 2):
        at = pl.multiple_of((me >> 1 ^ s >> 1) * 2 * rows, 2 * rows)
        for i, (a, b) in enumerate(zip(part_of(s), part_of(s + 1))):
            x = merge(low, a, b, 4)
            x = jnp.where(me & 1 == 0, x, pltpu.roll(x, rows, 0))
            x_scr[i, pl.ds(at, 2 * rows), :] = x

    block = pair_ref[...].reshape(rows * side, width)
    contracted = x_scr[...].reshape(rows * side, hidden)
    first = finish(
        block, contracted, gate_ref[...], gain_ref, shift_ref, out_w_ref, out_bias_ref, 0
    )
    first_ref[...] = first
    normed_ref[...] = normalize(first, gain_ref[1, 0:1, :], shift_ref[1, 0:1, :]).astype(BF16)


def add_pieces(pieces, left_scr, x_ref, start):
    rows, side, hidden = x_ref.shape
    for n, (piece, came) in enumerate(pieces):
        left_scr[n] = piece[rows * side :, :].astype(F32)

    def columns(at):
        totals = [start(i, at) for i in range(rows)]
        for n, (piece, came) in enumerate(pieces):
            for a in range(rows):
                right = piece[pl.ds(a * side + at, CHUNK), :].astype(F32)
                for i in range(rows):
                    row = a * 2 * rows + came * rows + i
                    totals[i] = totals[i] + left_scr[n, row : row + 1, :] * right
        for i in range(rows):
            x_ref[i, pl.ds(at, CHUNK), :] = totals[i]

    if side == CHUNK:
        columns(0)
    else:
        pl.loop(0, side // CHUNK)(lambda n: columns(pl.multiple_of(n * CHUNK, CHUNK)))


def form_incoming(held, me, normed, out_refs, mask_ref, edge_w_ref, edge_bias_ref, rows, side):
    chip = me >> 1
    hidden = out_refs[0].shape[1]
    columns, places = [], []
    for s, normed_ref, out_ref in zip(held, normed, out_refs):
        edges(
            normed_ref, out_ref.at[pl.ds(0, rows * side)], (me ^ s) * rows, side,
            mask_ref, edge_w_ref, edge_bias_ref, 1, 2,
        )
        for a in range(rows):
            both = normed_ref[pl.ds(pl.multiple_of(a * side + (chip >> 1) * 16, 16), 16), :]
            both = both.astype(F32)
            columns.append(jnp.where(chip & 1 == 0, both[:8], both[8:]))
            places.append(jnp.full((8, hidden), (me ^ s) * rows + a, jnp.int32))
    left = gated(
        jnp.concatenate(columns, 0).astype(BF16), edge_w_ref, edge_bias_ref, 1, 0, hidden
    )
    column = chip * 8 + lax.broadcasted_iota(jnp.int32, left.shape, 0) % 8
    left = masked(left, jnp.concatenate(places, 0), column, mask_ref)
    left = left.reshape(len(held) * rows, 8, hidden)
    left = jnp.where(me & 1 == 0, left, pltpu.roll(left, rows, 1))
    left = left.reshape(len(held), rows * 8, hidden).astype(BF16)
    for n, out_ref in enumerate(out_refs):
        out_ref[rows * side :, :] = left[n]


def incoming_edges_kernel(held, at_ref, *refs):
    normed, refs = refs[: len(held)], refs[len(held) :]
    mask_ref, edge_w_ref, edge_bias_ref, *refs = refs
    if held[0] == 0:
        out_ref, x_ref, gate_ref, left_scr = refs
        gate_of(normed[0], gate_ref, edge_w_ref, edge_bias_ref, 1)
    else:
        before_ref, out_ref, x_ref, left_scr = refs
    rows, side, hidden = x_ref.shape
    outs = [out_ref.at[n] for n in range(len(held))]
    form_incoming(
        held, at_ref[0], normed, outs, mask_ref, edge_w_ref, edge_bias_ref, rows, side
    )

    def start(i, at):
        if held[0] == 0:
            return jnp.zeros((CHUNK, hidden), F32)
        return before_ref[i, pl.ds(at, CHUNK), :]

    add_pieces([(out, 0) for out in outs], left_scr, x_ref, start)


def incoming_last_kernel(last, rows, at_ref, normed_ref, mask_ref, edge_w_ref, edge_bias_ref, *refs):
    before_ref, out_ref = refs
    count = before_ref.shape[0]
    out_ref[:count] = before_ref[...]
    form_incoming(
        [last], at_ref[0], [normed_ref], [out_ref.at[count]],
        mask_ref, edge_w_ref, edge_bias_ref, rows, normed_ref.shape[0] // rows,
    )


def incoming_kernel(before_ref, piece_ref, last_ref, x_ref, left_scr):
    pieces = [(piece_ref.at[n], 1) for n in range(piece_ref.shape[0])]
    pieces.append((last_ref.at[last_ref.shape[0] - 1], 0))
    add_pieces(pieces, left_scr, x_ref, lambda i, at: before_ref[i, pl.ds(at, CHUNK), :])


def incoming_finish_kernel(
    before_ref, piece_ref, first_ref, gate_ref, gain_ref, shift_ref, out_w_ref, out_bias_ref,
    out_ref, left_scr, x_scr,
):
    rows, side, width = out_ref.shape
    hidden = gate_ref.shape[1]
    pieces = [(piece_ref.at[n], 1) for n in range(piece_ref.shape[0])]
    add_pieces(pieces, left_scr, x_scr, lambda i, at: before_ref[i, pl.ds(at, CHUNK), :])
    out_ref[...] = finish(
        first_ref[...], x_scr[...].reshape(rows * side, hidden), gate_ref[...],
        gain_ref, shift_ref, out_w_ref, out_bias_ref, 1,
    ).reshape(rows, side, width)


def call(kernel, name, outs, *operands, scalar=None, scratch=(), flops=0):
    given = operands if scalar is None else (scalar, *operands)
    cost = pl.CostEstimate(flops=flops, bytes_accessed=flops // 64, transcendentals=0)
    return pl.pallas_call(
        kernel,
        in_specs=[SMEM] * (scalar is not None) + [VMEM] * len(operands),
        out_specs=[VMEM] * len(outs),
        out_shape=[jax.ShapeDtypeStruct(*out) for out in outs],
        scratch_shapes=[pltpu.VMEM(*one) for one in scratch],
        compiler_params=PARAMS,
        cost_estimate=cost if flops else None,
        name=name,
    )(*given)


def body(pair, residue_mask, norm_gain, norm_bias, edge_w, edge_bias, out_w, out_bias):
    rows, side, width = pair.shape
    hidden = out_w.shape[1]
    dap = lax.axis_size("dap")
    planes = dap // PLANE
    me = lax.axis_index("dap").reshape(1)
    mask = residue_mask.reshape(1, side)
    count = rows * side
    arguments = (pair, norm_gain, norm_bias, mask, edge_w, edge_bias, out_w, out_bias)
    *kept, normed = pl.pallas_call(
        norm_kernel,
        in_specs=[pl.BlockSpec(memory_space=pltpu.HBM)] * len(arguments),
        out_specs=[VMEM] * (len(arguments) + 1),
        out_shape=[jax.ShapeDtypeStruct(value.shape, value.dtype) for value in arguments]
        + [jax.ShapeDtypeStruct((count, width), BF16)],
        scratch_shapes=[pltpu.SemaphoreType.DMA((len(arguments),))],
        compiler_params=PARAMS,
        name="norm",
    )(*[pltpu.with_memory_space_constraint(value, pltpu.HBM) for value in arguments])
    pair, norm_gain, norm_bias, mask, edge_w, edge_bias, out_w, out_bias = kept
    norms = (norm_gain, norm_bias)
    weights = (mask, edge_w, edge_bias)
    span = count + 2 * rows * rows

    def swap(piece, bits):
        return lax.ppermute(piece, "dap", [(device, device ^ bits) for device in range(dap)])

    def gather(own):
        pieces = {0: own, 2: swap(own, 2)}
        for k in range(planes - 1, 0, -1):
            pieces[PLANE * k] = swap(own, PLANE * k)
        for k in range(planes - 1, 0, -1):
            pieces[PLANE * k + 2] = swap(pieces[PLANE * k], 2)
        return pieces

    groups = (
        [PLANE * k for k in range(planes)],
        [2] + [PLANE * k + 2 for k in range(planes - 1, 0, -1) if k != 2],
    )
    last = PLANE * min(2, planes - 1) + 2
    came = [[s ^ 1 for s in groups[0]], [s ^ 1 for s in groups[1] + [last]]]

    def work(pieces):
        return 2 * pieces * count * rows * hidden

    pieces = gather(normed)
    others, parts = [], []
    for group in groups:
        held = len(group)
        outs = [((held, count, hidden), BF16), ((held, rows, 8, hidden), F32)]
        if group[0] == 0:
            outs += [((count, hidden), F32), ((count, width), F32)]
        right, part, *rest = call(
            functools.partial(outgoing_edges_kernel, group, rows),
            "outgoing_edges", outs, *[pieces[s] for s in group], *weights,
            *([left] if group[0] else []), scalar=me, flops=work(held),
        )
        if rest:
            left, gate = rest
        parts.append(part)
        if group[0] == 0:
            others.append(swap(right, 1))
    (right,) = call(
        functools.partial(outgoing_last_kernel, last, rows), "outgoing_last",
        [((planes, count, hidden), BF16)], pieces[last], *weights, right, scalar=me,
    )
    others.append(swap(right, 1))
    known = [*groups, came[0] + [last]]
    (part,) = call(
        outgoing_kernel, "outgoing", [((planes + 1, rows, 8, hidden), F32)],
        left, others[0], right, flops=work(planes + 1),
    )
    first, normed = call(
        functools.partial(outgoing_finish_kernel, came[1], known), "outgoing_finish",
        [((count, width), F32), ((count, width), BF16)],
        others[1], *parts, part, left, gate, pair, *norms, out_w, out_bias,
        scalar=me, scratch=[((rows, side, hidden), F32)],
    )

    pieces = gather(normed)
    others, x = [], []
    for group in groups:
        held = len(group)
        outs = [((held, span, hidden), BF16), ((rows, side, hidden), F32)]
        if group[0] == 0:
            outs += [((count, width), F32)]
        edge, *x = call(
            functools.partial(incoming_edges_kernel, group),
            "incoming_edges", outs, *[pieces[s] for s in group], *weights, *x,
            scalar=me, scratch=[((held, 2 * rows * rows, hidden), F32)], flops=work(held),
        )
        if group[0] == 0:
            gate = x.pop()
            others.append(swap(edge, 1))
    (edge,) = call(
        functools.partial(incoming_last_kernel, last, rows), "incoming_last",
        [((planes, span, hidden), BF16)], pieces[last], *weights, edge, scalar=me,
    )
    others.append(swap(edge, 1))
    x = call(
        incoming_kernel, "incoming", [((rows, side, hidden), F32)], *x, others[0], edge,
        scratch=[((planes + 1, 2 * rows * rows, hidden), F32)], flops=work(planes + 1),
    )
    (out,) = call(
        incoming_finish_kernel, "incoming_finish", [(pair.shape, F32)],
        *x, others[1], first, gate, *norms, out_w, out_bias,
        scratch=[((planes, 2 * rows * rows, hidden), F32), ((rows, side, hidden), F32)],
    )
    return out


def solution(mesh):
    in_specs = (P(("groups", "dap"), None, None), P("groups"), P(), P(), P(), P(), P(), P())
    out_specs = P(("groups", "dap"), None, None)
    return jax.shard_map(body, mesh=mesh, in_specs=in_specs, out_specs=out_specs, check_vma=False)
```

```python
import functools

import jax
import jax.numpy as jnp
from jax import lax
from jax.experimental import pallas as pl
from jax.experimental.pallas import tpu as pltpu
from jax.sharding import PartitionSpec as P

F32 = jnp.float32
BF16 = jnp.bfloat16
VMEM = pl.BlockSpec(memory_space=pltpu.VMEM)
SMEM = pl.BlockSpec(memory_space=pltpu.SMEM)
PLANE = 4
CHUNK = 64
BLOCK = 256
PARAMS = pltpu.CompilerParams(vmem_limit_bytes=48 * 1024 * 1024)


def source(me, s):
    turn = PLANE if s >= 2 * PLANE else 0
    return me ^ s ^ ((me ^ s) & 1) * turn


def normalize(values, gain, shift):
    mean = jnp.mean(values, axis=-1, keepdims=True)
    centered = values - mean
    spread = jnp.mean(centered * centered, axis=-1, keepdims=True)
    return centered * lax.rsqrt(spread + 1e-05) * gain + shift


def sigmoid(values):
    return 0.5 * jnp.tanh(0.5 * values) + 0.5


def gated(normed, edge_w_ref, edge_bias_ref, layer, index, hidden):
    span = slice(index * hidden, (index + 2) * hidden)
    both = jnp.dot(normed, edge_w_ref[layer, :, span], preferred_element_type=F32)
    both = both + edge_bias_ref[layer : layer + 1, span]
    return sigmoid(both[:, :hidden]) * both[:, hidden:]


def masked(values, row, column, mask_ref):
    valid = jnp.sum(mask_ref[...].astype(F32), axis=1, keepdims=True)
    return jnp.where(jnp.maximum(row, column).astype(F32) < valid, values, 0.0)


def edges(normed_ref, out_ref, first_row, side, mask_ref, edge_w_ref, edge_bias_ref, layer, index):
    count, hidden = normed_ref.shape[0], out_ref.shape[1]
    size = min(count, BLOCK)

    def block(at):
        values = gated(
            normed_ref[pl.ds(at, size), :], edge_w_ref, edge_bias_ref, layer, index, hidden
        )
        position = at + lax.broadcasted_iota(jnp.int32, values.shape, 0)
        values = masked(values, first_row + position // side, position % side, mask_ref)
        out_ref[pl.ds(at, size), :] = values.astype(BF16).astype(out_ref.dtype)

    if count == size:
        block(0)
    else:
        pl.loop(0, count // size)(lambda n: block(pl.multiple_of(n * size, size)))


def gate_of(normed_ref, gate_ref, edge_w_ref, edge_bias_ref, layer):
    width = gate_ref.shape[1]
    low = edge_bias_ref.shape[1] - width
    value = jnp.dot(normed_ref[...], edge_w_ref[layer, :, low:], preferred_element_type=F32)
    gate_ref[...] = sigmoid(value + edge_bias_ref[layer : layer + 1, low:])


def finish(block, contracted, gate, gain_ref, shift_ref, out_w_ref, out_bias_ref, layer):
    normed = normalize(contracted, gain_ref[layer, 1:2, :], shift_ref[layer, 1:2, :]).astype(BF16)
    result = jnp.dot(normed, out_w_ref[layer], preferred_element_type=F32)
    return block + gate * (result + out_bias_ref[layer : layer + 1, :])


def norm_kernel(*refs):
    count = len(refs) // 2 - 1
    given, kept, (normed_ref, sems) = refs[:count], refs[count : 2 * count], refs[2 * count :]
    copies = [
        pltpu.make_async_copy(source, target, sems.at[n])
        for n, (source, target) in enumerate(zip(given, kept))
    ]
    for copy in copies:
        copy.start()
    for copy in copies[:3]:
        copy.wait()
    pair_ref, gain_ref, shift_ref = kept[:3]
    block = pair_ref[...].reshape(normed_ref.shape)
    normed_ref[...] = normalize(block, gain_ref[0, 0:1, :], shift_ref[0, 0:1, :]).astype(BF16)
    for copy in copies[3:]:
        copy.wait()


def merge(low, a, b, shift):
    return jnp.where(low, a, b) + pltpu.roll(jnp.where(low, b, a), shift, 0)


def fold(parts, sub):
    low = (sub & 1) == 0
    first, second = merge(low, parts[0], parts[1], 1), merge(low, parts[2], parts[3], 1)
    return merge((sub & 2) == 0, first, second, 2)


def row_sums(left_ref, piece_ref, a, rows, side):
    hidden = left_ref.shape[1]

    def chunk(at, totals):
        right = piece_ref[pl.ds(a * side + at, CHUNK), :].astype(F32)
        sums = []
        for i in range(rows):
            product = left_ref[pl.ds(i * side + at, CHUNK), :] * right
            sums.append(jnp.sum(product.reshape(CHUNK // 8, 8, hidden), axis=0))
        return [t + s for t, s in zip(totals, sums)] if totals else sums

    totals = chunk(0, None)
    if side > CHUNK:
        totals = lax.fori_loop(
            1, side // CHUNK, lambda n, t: chunk(pl.multiple_of(n * CHUNK, CHUNK), t), totals
        )
    return totals


def piece_products(left_ref, piece_ref, rows, side):
    sub = lax.broadcasted_iota(jnp.int32, (8, left_ref.shape[1]), 0)
    totals = [row_sums(left_ref, piece_ref, a, rows, side) for a in range(rows)]
    return [fold([totals[a][i] for a in range(rows)], sub) for i in range(rows)]


def outgoing_edges_kernel(held, rows, at_ref, *refs):
    normed, refs = refs[: len(held)], refs[len(held) :]
    mask_ref, edge_w_ref, edge_bias_ref, *refs = refs
    own = held[0] == 0
    if own:
        right_ref, part_ref, left_ref, gate_ref = refs
    else:
        left_ref, right_ref, part_ref = refs
    side = left_ref.shape[0] // rows
    shared = (side, mask_ref, edge_w_ref, edge_bias_ref, 0)
    if own:
        edges(normed[0], left_ref, at_ref[0] * rows, *shared, 0)
        gate_of(normed[0], gate_ref, edge_w_ref, edge_bias_ref, 0)
    for n, s in enumerate(held):
        edges(normed[n], right_ref.at[n], source(at_ref[0], s) * rows, *shared, 2)
        for i, part in enumerate(piece_products(left_ref, right_ref.at[n], rows, side)):
            part_ref[n, i] = part


def outgoing_last_kernel(last, rows, at_ref, normed_ref, mask_ref, edge_w_ref, edge_bias_ref, *refs):
    before_ref, right_ref = refs
    count = before_ref.shape[0]
    side = normed_ref.shape[0] // rows
    right_ref[:count] = before_ref[...]
    edges(
        normed_ref, right_ref.at[count], source(at_ref[0], last) * rows, side,
        mask_ref, edge_w_ref, edge_bias_ref, 0, 2,
    )


def outgoing_kernel(left_ref, piece_ref, last_ref, part_ref):
    rows = part_ref.shape[1]
    side = left_ref.shape[0] // rows
    count = piece_ref.shape[0]
    pieces = [piece_ref.at[n] for n in range(count)] + [last_ref.at[last_ref.shape[0] - 1]]
    for n, piece in enumerate(pieces):
        for i, part in enumerate(piece_products(left_ref, piece, rows, side)):
            part_ref[n, i] = part


def outgoing_finish_kernel(last, given, at_ref, piece_ref, *refs):
    parts, refs = refs[: len(given)], refs[len(given) :]
    (
        left_ref, gate_ref, pair_ref, gain_ref, shift_ref, out_w_ref, out_bias_ref,
        first_ref, normed_ref, x_scr,
    ) = refs
    rows, side, width = pair_ref.shape
    hidden = left_ref.shape[1]
    sub = lax.broadcasted_iota(jnp.int32, (8, hidden), 0)
    me = at_ref[0]
    low = (sub & 4) == 0
    known = {s: (ref, n) for ref, held in zip(parts, given) for n, s in enumerate(held)}

    def part_of(s):
        if s in last:
            return piece_products(left_ref, piece_ref.at[last.index(s)], rows, side)
        ref, n = known[s]
        return [ref[n, i] for i in range(rows)]

    for s in range(0, len(known) + len(last), 2):
        at = pl.multiple_of((source(me, s) >> 1) * 2 * rows, 2 * rows)
        other = s + 1 if s < 2 * PLANE else (s ^ PLANE) + 1
        for i, (a, b) in enumerate(zip(part_of(s), part_of(other))):
            x = merge(low, a, b, 4)
            x = jnp.where(me & 1 == 0, x, pltpu.roll(x, rows, 0))
            x_scr[i, pl.ds(at, 2 * rows), :] = x

    block = pair_ref[...].reshape(rows * side, width)
    contracted = x_scr[...].reshape(rows * side, hidden)
    first = finish(
        block, contracted, gate_ref[...], gain_ref, shift_ref, out_w_ref, out_bias_ref, 0
    )
    first_ref[...] = first
    normed_ref[...] = normalize(first, gain_ref[1, 0:1, :], shift_ref[1, 0:1, :]).astype(BF16)


def add_pieces(pieces, left_scr, x_ref, start):
    rows, side, hidden = x_ref.shape
    for n, (piece, came) in enumerate(pieces):
        left_scr[n] = piece[rows * side :, :].astype(F32)

    def columns(at):
        totals = [start(i, at) for i in range(rows)]
        for n, (piece, came) in enumerate(pieces):
            for a in range(rows):
                right = piece[pl.ds(a * side + at, CHUNK), :].astype(F32)
                for i in range(rows):
                    row = a * 2 * rows + came * rows + i
                    totals[i] = totals[i] + left_scr[n, row : row + 1, :] * right
        for i in range(rows):
            x_ref[i, pl.ds(at, CHUNK), :] = totals[i]

    if side == CHUNK:
        columns(0)
    else:
        pl.loop(0, side // CHUNK)(lambda n: columns(pl.multiple_of(n * CHUNK, CHUNK)))


def form_incoming(held, me, normed, out_refs, mask_ref, edge_w_ref, edge_bias_ref, rows, side):
    chip = me >> 1
    hidden = out_refs[0].shape[1]
    columns, places = [], []
    for s, normed_ref, out_ref in zip(held, normed, out_refs):
        edges(
            normed_ref, out_ref.at[pl.ds(0, rows * side)], source(me, s) * rows, side,
            mask_ref, edge_w_ref, edge_bias_ref, 1, 2,
        )
        for a in range(rows):
            both = normed_ref[pl.ds(pl.multiple_of(a * side + (chip >> 1) * 16, 16), 16), :]
            both = both.astype(F32)
            columns.append(jnp.where(chip & 1 == 0, both[:8], both[8:]))
            places.append(jnp.full((8, hidden), source(me, s) * rows + a, jnp.int32))
    left = gated(
        jnp.concatenate(columns, 0).astype(BF16), edge_w_ref, edge_bias_ref, 1, 0, hidden
    )
    column = chip * 8 + lax.broadcasted_iota(jnp.int32, left.shape, 0) % 8
    left = masked(left, jnp.concatenate(places, 0), column, mask_ref)
    left = left.reshape(len(held) * rows, 8, hidden)
    left = jnp.where(me & 1 == 0, left, pltpu.roll(left, rows, 1))
    left = left.reshape(len(held), rows * 8, hidden).astype(BF16)
    for n, out_ref in enumerate(out_refs):
        out_ref[rows * side :, :] = left[n]


def incoming_edges_kernel(held, at_ref, *refs):
    normed, refs = refs[: len(held)], refs[len(held) :]
    mask_ref, edge_w_ref, edge_bias_ref, *refs = refs
    if held[0] == 0:
        out_ref, x_ref, gate_ref, left_scr = refs
        gate_of(normed[0], gate_ref, edge_w_ref, edge_bias_ref, 1)
    else:
        before_ref, out_ref, x_ref, left_scr = refs
    rows, side, hidden = x_ref.shape
    outs = [out_ref.at[n] for n in range(len(held))]
    form_incoming(
        held, at_ref[0], normed, outs, mask_ref, edge_w_ref, edge_bias_ref, rows, side
    )

    def start(i, at):
        if held[0] == 0:
            return jnp.zeros((CHUNK, hidden), F32)
        return before_ref[i, pl.ds(at, CHUNK), :]

    add_pieces([(out, 0) for out in outs], left_scr, x_ref, start)


def incoming_last_kernel(last, rows, at_ref, normed_ref, mask_ref, edge_w_ref, edge_bias_ref, *refs):
    before_ref, out_ref = refs
    count = before_ref.shape[0]
    out_ref[:count] = before_ref[...]
    form_incoming(
        [last], at_ref[0], [normed_ref], [out_ref.at[count]],
        mask_ref, edge_w_ref, edge_bias_ref, rows, normed_ref.shape[0] // rows,
    )


def incoming_kernel(before_ref, piece_ref, last_ref, x_ref, left_scr):
    pieces = [(piece_ref.at[n], 1) for n in range(piece_ref.shape[0])]
    pieces.append((last_ref.at[last_ref.shape[0] - 1], 0))
    add_pieces(pieces, left_scr, x_ref, lambda i, at: before_ref[i, pl.ds(at, CHUNK), :])


def incoming_finish_kernel(
    before_ref, piece_ref, first_ref, gate_ref, gain_ref, shift_ref, out_w_ref, out_bias_ref,
    out_ref, left_scr, x_scr,
):
    rows, side, width = out_ref.shape
    hidden = gate_ref.shape[1]
    pieces = [(piece_ref.at[n], 1) for n in range(piece_ref.shape[0])]
    add_pieces(pieces, left_scr, x_scr, lambda i, at: before_ref[i, pl.ds(at, CHUNK), :])
    out_ref[...] = finish(
        first_ref[...], x_scr[...].reshape(rows * side, hidden), gate_ref[...],
        gain_ref, shift_ref, out_w_ref, out_bias_ref, 1,
    ).reshape(rows, side, width)


def call(kernel, name, outs, *operands, scalar=None, scratch=(), flops=0):
    given = operands if scalar is None else (scalar, *operands)
    cost = pl.CostEstimate(flops=flops, bytes_accessed=flops // 64, transcendentals=0)
    return pl.pallas_call(
        kernel,
        in_specs=[SMEM] * (scalar is not None) + [VMEM] * len(operands),
        out_specs=[VMEM] * len(outs),
        out_shape=[jax.ShapeDtypeStruct(*out) for out in outs],
        scratch_shapes=[pltpu.VMEM(*one) for one in scratch],
        compiler_params=PARAMS,
        cost_estimate=cost if flops else None,
        name=name,
    )(*given)


def body(pair, residue_mask, norm_gain, norm_bias, edge_w, edge_bias, out_w, out_bias):
    rows, side, width = pair.shape
    hidden = out_w.shape[1]
    dap = lax.axis_size("dap")
    planes = dap // PLANE
    me = lax.axis_index("dap").reshape(1)
    mask = residue_mask.reshape(1, side)
    count = rows * side
    arguments = (pair, norm_gain, norm_bias, mask, edge_w, edge_bias, out_w, out_bias)
    *kept, normed = pl.pallas_call(
        norm_kernel,
        in_specs=[pl.BlockSpec(memory_space=pltpu.HBM)] * len(arguments),
        out_specs=[VMEM] * (len(arguments) + 1),
        out_shape=[jax.ShapeDtypeStruct(value.shape, value.dtype) for value in arguments]
        + [jax.ShapeDtypeStruct((count, width), BF16)],
        scratch_shapes=[pltpu.SemaphoreType.DMA((len(arguments),))],
        compiler_params=PARAMS,
        name="norm",
    )(*[pltpu.with_memory_space_constraint(value, pltpu.HBM) for value in arguments])
    pair, norm_gain, norm_bias, mask, edge_w, edge_bias, out_w, out_bias = kept
    norms = (norm_gain, norm_bias)
    weights = (mask, edge_w, edge_bias)
    span = count + 2 * rows * rows

    def swap(piece, s):
        return lax.ppermute(piece, "dap", [(source(device, s), device) for device in range(dap)])

    def gather(own):
        pieces = {0: own, 2: swap(own, 2)}
        for k in range(planes - 1, 0, -1):
            pieces[PLANE * k] = swap(own, PLANE * k)
        for k in range(planes - 1, 0, -1):
            pieces[PLANE * k + 2] = swap(pieces[PLANE * k], 2)
        return pieces

    groups = (
        [PLANE * k for k in range(planes)],
        [2] + [PLANE * k + 2 for k in range(planes - 1, 0, -1) if k != 2],
    )
    last = PLANE * min(2, planes - 1) + 2
    came = [[s ^ 1 for s in groups[0]], [s ^ 1 for s in groups[1] + [last]]]

    def work(pieces):
        return 2 * pieces * count * rows * hidden

    pieces = gather(normed)
    others, parts = [], []
    for group in groups:
        held = len(group)
        outs = [((held, count, hidden), BF16), ((held, rows, 8, hidden), F32)]
        if group[0] == 0:
            outs += [((count, hidden), F32), ((count, width), F32)]
        right, part, *rest = call(
            functools.partial(outgoing_edges_kernel, group, rows),
            "outgoing_edges", outs, *[pieces[s] for s in group], *weights,
            *([left] if group[0] else []), scalar=me, flops=work(held),
        )
        if rest:
            left, gate = rest
        parts.append(part)
        if group[0] == 0:
            others.append(swap(right, 1))
    (right,) = call(
        functools.partial(outgoing_last_kernel, last, rows), "outgoing_last",
        [((planes, count, hidden), BF16)], pieces[last], *weights, right, scalar=me,
    )
    others.append(swap(right, 1))
    known = [*groups, came[0] + [last]]
    (part,) = call(
        outgoing_kernel, "outgoing", [((planes + 1, rows, 8, hidden), F32)],
        left, others[0], right, flops=work(planes + 1),
    )
    first, normed = call(
        functools.partial(outgoing_finish_kernel, came[1], known), "outgoing_finish",
        [((count, width), F32), ((count, width), BF16)],
        others[1], *parts, part, left, gate, pair, *norms, out_w, out_bias,
        scalar=me, scratch=[((rows, side, hidden), F32)],
    )

    pieces = gather(normed)
    others, x = [], []
    for group in groups:
        held = len(group)
        outs = [((held, span, hidden), BF16), ((rows, side, hidden), F32)]
        if group[0] == 0:
            outs += [((count, width), F32)]
        edge, *x = call(
            functools.partial(incoming_edges_kernel, group),
            "incoming_edges", outs, *[pieces[s] for s in group], *weights, *x,
            scalar=me, scratch=[((held, 2 * rows * rows, hidden), F32)], flops=work(held),
        )
        if group[0] == 0:
            gate = x.pop()
            others.append(swap(edge, 1))
    (edge,) = call(
        functools.partial(incoming_last_kernel, last, rows), "incoming_last",
        [((planes, span, hidden), BF16)], pieces[last], *weights, edge, scalar=me,
    )
    others.append(swap(edge, 1))
    x = call(
        incoming_kernel, "incoming", [((rows, side, hidden), F32)], *x, others[0], edge,
        scratch=[((planes + 1, 2 * rows * rows, hidden), F32)], flops=work(planes + 1),
    )
    (out,) = call(
        incoming_finish_kernel, "incoming_finish", [(pair.shape, F32)],
        *x, others[1], first, gate, *norms, out_w, out_bias,
        scratch=[((planes, 2 * rows * rows, hidden), F32), ((rows, side, hidden), F32)],
    )
    return out


def solution(mesh):
    in_specs = (P(("groups", "dap"), None, None), P("groups"), P(), P(), P(), P(), P(), P())
    out_specs = P(("groups", "dap"), None, None)
    return jax.shard_map(body, mesh=mesh, in_specs=in_specs, out_specs=out_specs, check_vma=False)
```

```python
import functools

import jax
import jax.numpy as jnp
from jax import lax
from jax.experimental import pallas as pl
from jax.experimental.pallas import tpu as pltpu
from jax.sharding import PartitionSpec as P

F32 = jnp.float32
BF16 = jnp.bfloat16
VMEM = pl.BlockSpec(memory_space=pltpu.VMEM)
SMEM = pl.BlockSpec(memory_space=pltpu.SMEM)
CHUNK = 64
BLOCK = 512
PARAMS = pltpu.CompilerParams(vmem_limit_bytes=48 * 1024 * 1024)


def normalize(values, gain, shift):
    mean = jnp.mean(values, axis=-1, keepdims=True)
    centered = values - mean
    spread = jnp.mean(centered * centered, axis=-1, keepdims=True)
    return centered * lax.rsqrt(spread + 1e-05) * gain + shift


def sigmoid(values):
    return 0.5 * jnp.tanh(0.5 * values) + 0.5


def gated(normed, edge_w_ref, edge_bias_ref, layer, index, hidden):
    span = slice(index * hidden, (index + 2) * hidden)
    both = jnp.dot(normed, edge_w_ref[layer, :, span], preferred_element_type=F32)
    both = both + edge_bias_ref[layer : layer + 1, span]
    return sigmoid(both[:, :hidden]) * both[:, hidden:]


def masked(values, row, column, mask_ref):
    valid = jnp.sum(mask_ref[...].astype(F32), axis=1, keepdims=True)
    return jnp.where(jnp.maximum(row, column).astype(F32) < valid, values, 0.0)


def edges(normed_ref, out_ref, first_row, side, mask_ref, edge_w_ref, edge_bias_ref, layer, index):
    count, hidden = normed_ref.shape[0], out_ref.shape[1]
    size = min(count, BLOCK)

    def block(at):
        values = gated(
            normed_ref[pl.ds(at, size), :], edge_w_ref, edge_bias_ref, layer, index, hidden
        )
        position = at + lax.broadcasted_iota(jnp.int32, values.shape, 0)
        values = masked(values, first_row + position // side, position % side, mask_ref)
        out_ref[pl.ds(at, size), :] = values.astype(BF16).astype(out_ref.dtype)

    if count == size:
        block(0)
    else:
        pl.loop(0, count // size)(lambda n: block(pl.multiple_of(n * size, size)))


def gate_of(normed, gate_ref, edge_w_ref, edge_bias_ref, layer):
    width = gate_ref.shape[1]
    low = edge_bias_ref.shape[1] - width
    value = jnp.dot(normed, edge_w_ref[layer, :, low:], preferred_element_type=F32)
    gate_ref[...] = sigmoid(value + edge_bias_ref[layer : layer + 1, low:])


def finish(block, contracted, gate, gain_ref, shift_ref, out_w_ref, out_bias_ref, layer):
    normed = normalize(contracted, gain_ref[layer, 1:2, :], shift_ref[layer, 1:2, :]).astype(BF16)
    result = jnp.dot(normed, out_w_ref[layer], preferred_element_type=F32)
    return block + gate * (result + out_bias_ref[layer : layer + 1, :])


def chip_of(me, distances, own):
    core = me & 1 if own else 1 - (me & 1)
    near, far = distances
    return me >> 1 ^ near + (far - near) * core


def load_kernel(*refs):
    count = len(refs) // 2
    given, kept, sems = refs[:count], refs[count : 2 * count], refs[2 * count]
    copies = [
        pltpu.make_async_copy(source, target, sems.at[n])
        for n, (source, target) in enumerate(zip(given, kept))
    ]
    for copy in copies:
        copy.start()
    for copy in copies:
        copy.wait()


def norm_kernel(at_ref, pair_ref, other_ref, gain_ref, shift_ref, both_ref, normed_ref):
    rows = pair_ref.shape[0]
    core = at_ref[0] & 1
    both_ref[pl.ds(core * rows, rows)] = pair_ref[...]
    both_ref[pl.ds((1 - core) * rows, rows)] = other_ref[...]
    block = both_ref[...].reshape(normed_ref.shape)
    normed_ref[...] = normalize(block, gain_ref[0, 0:1, :], shift_ref[0, 0:1, :]).astype(BF16)


def merge(low, a, b, shift):
    return jnp.where(low, a, b) + pltpu.roll(jnp.where(low, b, a), shift, 0)


def fold(parts, sub):
    for shift in (1, 2, 4):
        low = (sub & shift) == 0
        parts = [merge(low, a, b, shift) for a, b in zip(parts[0::2], parts[1::2])]
    return parts[0]


def row_sums(left_ref, piece_ref, a, first, some, side):
    hidden = left_ref.shape[1]

    def chunk(at, totals):
        right = piece_ref[pl.ds(a * side + at, CHUNK), :].astype(F32)
        sums = []
        for i in range(first, first + some):
            product = left_ref[pl.ds(i * side + at, CHUNK), :] * right
            sums.append(jnp.sum(product.reshape(CHUNK // 8, 8, hidden), axis=0))
        return [t + s for t, s in zip(totals, sums)] if totals else sums

    totals = chunk(0, None)
    if side > CHUNK:
        totals = lax.fori_loop(
            1, side // CHUNK, lambda n, t: chunk(pl.multiple_of(n * CHUNK, CHUNK), t), totals
        )
    return totals


def products(left_ref, piece_ref, part_ref, side):
    rows, height, hidden = part_ref.shape
    sub = lax.broadcasted_iota(jnp.int32, (height, hidden), 0)
    some = 4
    for first in range(0, rows, some):
        totals = [row_sums(left_ref, piece_ref, a, first, some, side) for a in range(height)]
        for i in range(some):
            part_ref[first + i] = fold([total[i] for total in totals], sub)


def outgoing_edges_kernel(held, side, at_ref, *refs):
    normed, refs = refs[: len(held)], refs[len(held) :]
    mask_ref, edge_w_ref, edge_bias_ref, *refs = refs
    if len(refs) == 5:
        own_ref, right_ref, part_ref, left_ref, gate_ref = refs
    else:
        left_ref, right_ref, part_ref = refs
    me = at_ref[0]
    height = left_ref.shape[0] // side
    shared = (side, mask_ref, edge_w_ref, edge_bias_ref, 0)
    if len(refs) == 5:
        edges(own_ref, left_ref, (me >> 1) * height, *shared, 0)
        gate_of(own_ref[...], gate_ref, edge_w_ref, edge_bias_ref, 0)
    for n, distances in enumerate(held):
        first = chip_of(me, distances, True) * height
        edges(normed[n], right_ref.at[n], first, *shared, 2)
        products(left_ref, right_ref.at[n], part_ref.at[n], side)


def outgoing_last_kernel(
    last, side, at_ref, normed_ref, mask_ref, edge_w_ref, edge_bias_ref, before_ref, right_ref
):
    count = before_ref.shape[0]
    height = normed_ref.shape[0] // side
    right_ref[:count] = before_ref[...]
    edges(
        normed_ref, right_ref.at[count], chip_of(at_ref[0], last, True) * height, side,
        mask_ref, edge_w_ref, edge_bias_ref, 0, 2,
    )


def outgoing_kernel(left_ref, piece_ref, last_ref, part_ref):
    side = left_ref.shape[0] // part_ref.shape[1]
    count = piece_ref.shape[0]
    pieces = [piece_ref.at[n] for n in range(count)] + [last_ref.at[last_ref.shape[0] - 1]]
    for n, piece in enumerate(pieces):
        products(left_ref, piece, part_ref.at[n], side)


def outgoing_finish_kernel(held, given, at_ref, piece_ref, *refs):
    parts, refs = refs[: len(given)], refs[len(given) :]
    (
        left_ref, gate_ref, both_ref, gain_ref, shift_ref, out_w_ref, out_bias_ref,
        first_ref, normed_ref, x_scr, part_scr,
    ) = refs
    height, side, width = both_ref.shape
    hidden = left_ref.shape[1]
    me = at_ref[0]

    def put(part, distances, own):
        at = pl.multiple_of(chip_of(me, distances, own) * height, height)
        for i in range(height):
            x_scr[i, pl.ds(at, height), :] = part[i]

    for part, slots in zip(parts, given):
        for n, (distances, own) in enumerate(slots):
            put(part.at[n], distances, own)
    for n, distances in enumerate(held):
        products(left_ref, piece_ref.at[n], part_scr.at[n], side)
        put(part_scr.at[n], distances, False)

    block = both_ref[...].reshape(height * side, width)
    contracted = x_scr[...].reshape(height * side, hidden)
    first = finish(
        block, contracted, gate_ref[...], gain_ref, shift_ref, out_w_ref, out_bias_ref, 0
    )
    first_ref[...] = first.reshape(first_ref.shape)
    normed_ref[...] = normalize(first, gain_ref[1, 0:1, :], shift_ref[1, 0:1, :]).astype(BF16)


def add_pieces(pieces, left_scr, x_ref, start):
    rows, side, hidden = x_ref.shape
    height = 2 * rows
    for n, (piece, came) in enumerate(pieces):
        left_scr[n] = piece[height * side :, :].astype(F32)

    def columns(at):
        totals = [start(i, at) for i in range(rows)]
        for n, (piece, came) in enumerate(pieces):
            for a in range(height):
                right = piece[pl.ds(a * side + at, CHUNK), :].astype(F32)
                for i in range(rows):
                    row = a * height + came * rows + i
                    totals[i] = totals[i] + left_scr[n, row : row + 1, :] * right
        for i in range(rows):
            x_ref[i, pl.ds(at, CHUNK), :] = totals[i]

    if side == CHUNK:
        columns(0)
    else:
        pl.loop(0, side // CHUNK)(lambda n: columns(pl.multiple_of(n * CHUNK, CHUNK)))


def form_incoming(held, me, normed, out_refs, mask_ref, edge_w_ref, edge_bias_ref, side):
    chip = me >> 1
    height = normed[0].shape[0] // side
    hidden = out_refs[0].shape[1]
    columns, places = [], []
    for distances, normed_ref, out_ref in zip(held, normed, out_refs):
        first = chip_of(me, distances, True) * height
        edges(
            normed_ref, out_ref.at[pl.ds(0, height * side)], first, side,
            mask_ref, edge_w_ref, edge_bias_ref, 1, 2,
        )
        for a in range(height):
            both = normed_ref[pl.ds(pl.multiple_of(a * side + (chip >> 1) * 16, 16), 16), :]
            both = both.astype(F32)
            columns.append(jnp.where(chip & 1 == 0, both[:8], both[8:]))
            places.append(jnp.full((8, hidden), first + a, jnp.int32))
    left = gated(
        jnp.concatenate(columns, 0).astype(BF16), edge_w_ref, edge_bias_ref, 1, 0, hidden
    )
    column = chip * 8 + lax.broadcasted_iota(jnp.int32, left.shape, 0) % 8
    left = masked(left, jnp.concatenate(places, 0), column, mask_ref)
    left = left.reshape(len(held) * height, 8, hidden)
    left = jnp.where(me & 1 == 0, left, pltpu.roll(left, 4, 1))
    left = left.reshape(len(held), height * 8, hidden).astype(BF16)
    for n, out_ref in enumerate(out_refs):
        out_ref[height * side :, :] = left[n]


def incoming_edges_kernel(held, side, at_ref, *refs):
    normed, refs = refs[: len(held)], refs[len(held) :]
    mask_ref, edge_w_ref, edge_bias_ref, extra_ref, out_ref, x_ref, *refs = refs
    rows, _, hidden = x_ref.shape
    me = at_ref[0]
    if len(refs) == 2:
        gate_ref, left_scr = refs
        count = rows * side
        own = extra_ref[pl.ds(pl.multiple_of((me & 1) * count, count), count), :]
        gate_of(own, gate_ref, edge_w_ref, edge_bias_ref, 1)
        start = lambda i, at: jnp.zeros((CHUNK, hidden), F32)
    else:
        (left_scr,) = refs
        start = lambda i, at: extra_ref[i, pl.ds(at, CHUNK), :]
    outs = [out_ref.at[n] for n in range(len(held))]
    form_incoming(held, me, normed, outs, mask_ref, edge_w_ref, edge_bias_ref, side)
    add_pieces([(out, 0) for out in outs], left_scr, x_ref, start)


def incoming_last_kernel(
    last, side, at_ref, normed_ref, mask_ref, edge_w_ref, edge_bias_ref, before_ref, out_ref
):
    count = before_ref.shape[0]
    out_ref[:count] = before_ref[...]
    form_incoming(
        [last], at_ref[0], [normed_ref], [out_ref.at[count]],
        mask_ref, edge_w_ref, edge_bias_ref, side,
    )


def incoming_kernel(before_ref, piece_ref, last_ref, x_ref, left_scr):
    pieces = [(piece_ref.at[n], 1) for n in range(piece_ref.shape[0])]
    pieces.append((last_ref.at[last_ref.shape[0] - 1], 0))
    add_pieces(pieces, left_scr, x_ref, lambda i, at: before_ref[i, pl.ds(at, CHUNK), :])


def incoming_finish_kernel(
    at_ref, before_ref, piece_ref, first_ref, gate_ref, gain_ref, shift_ref, out_w_ref,
    out_bias_ref, out_ref, left_scr, x_scr,
):
    rows, side, width = out_ref.shape
    hidden = gate_ref.shape[1]
    pieces = [(piece_ref.at[n], 1) for n in range(piece_ref.shape[0])]
    add_pieces(pieces, left_scr, x_scr, lambda i, at: before_ref[i, pl.ds(at, CHUNK), :])
    first = first_ref[pl.ds((at_ref[0] & 1) * rows, rows)].reshape(rows * side, width)
    out_ref[...] = finish(
        first, x_scr[...].reshape(rows * side, hidden), gate_ref[...],
        gain_ref, shift_ref, out_w_ref, out_bias_ref, 1,
    ).reshape(rows, side, width)


def call(kernel, name, outs, *operands, scalar=None, scratch=()):
    given = operands if scalar is None else (scalar, *operands)
    return pl.pallas_call(
        kernel,
        in_specs=[SMEM] * (scalar is not None) + [VMEM] * len(operands),
        out_specs=[VMEM] * len(outs),
        out_shape=[jax.ShapeDtypeStruct(*out) for out in outs],
        scratch_shapes=[pltpu.VMEM(*one) for one in scratch],
        compiler_params=PARAMS,
        name=name,
    )(*given)


def body(pair, residue_mask, norm_gain, norm_bias, edge_w, edge_bias, out_w, out_bias):
    rows, side, width = pair.shape
    hidden = out_w.shape[1]
    dap = lax.axis_size("dap")
    chips = dap // 2
    me = lax.axis_index("dap").reshape(1)
    mask = residue_mask.reshape(1, side)
    height = 2 * rows
    count = height * side
    span = count + height * height
    half = chips // 2
    quarter = half // 2

    near = [n for n in range(half) if n % 4 in (1, 2)]
    far = [half + n for n in range(half - 2, -1, -2)]
    slots = list(zip(near, far))
    slots += [(a ^ 2, b ^ 1) for a, b in slots]
    groups = (list(range(quarter)), list(range(half - 1, quarter, -1)))
    last = quarter

    def swap(piece, distances):
        pairs = [(device, device ^ 2 * distances[device & 1]) for device in range(dap)]
        return lax.ppermute(piece, "dap", pairs)

    def flip(value):
        return lax.ppermute(value, "dap", [(device, device ^ 1) for device in range(dap)])

    def gather(own):
        pieces = [swap(own, distances) for distances in slots[:quarter]]
        return pieces + [swap(piece, (2, 1)) for piece in pieces]

    arguments = (pair, norm_gain, norm_bias, mask, edge_w, edge_bias, out_w, out_bias)
    kept = pl.pallas_call(
        load_kernel,
        in_specs=[pl.BlockSpec(memory_space=pltpu.HBM)] * len(arguments),
        out_specs=[VMEM] * len(arguments),
        out_shape=[jax.ShapeDtypeStruct(value.shape, value.dtype) for value in arguments],
        scratch_shapes=[pltpu.SemaphoreType.DMA((len(arguments),))],
        compiler_params=PARAMS,
        name="load",
    )(*[pltpu.with_memory_space_constraint(value, pltpu.HBM) for value in arguments])
    other = flip(pair)
    pair, norm_gain, norm_bias, mask, edge_w, edge_bias, out_w, out_bias = kept
    norms = (norm_gain, norm_bias)
    weights = (mask, edge_w, edge_bias)
    part_shape = (height, height, hidden)
    x_shape = (rows, side, hidden)

    both, normed = call(
        norm_kernel, "norm", [((height, side, width), F32), ((count, width), BF16)],
        pair, other, *norms, scalar=me,
    )
    pieces = gather(normed)
    others, parts = [], []
    for group in groups:
        held = [slots[n] for n in group]
        outs = [((len(held), count, hidden), BF16), ((len(held), *part_shape), F32)]
        if not parts:
            outs += [((count, hidden), F32), ((count, width), F32)]
        right, part, *rest = call(
            functools.partial(outgoing_edges_kernel, held, side), "outgoing_edges", outs,
            *[pieces[n] for n in group], *weights, left if parts else normed, scalar=me,
        )
        if rest:
            left, gate = rest
            others.append(flip(right))
        parts.append(part)
    (right,) = call(
        functools.partial(outgoing_last_kernel, slots[last], side), "outgoing_last",
        [((quarter, count, hidden), BF16)], pieces[last], *weights, right, scalar=me,
    )
    others.append(flip(right))
    (part,) = call(
        outgoing_kernel, "outgoing", [((quarter + 1, *part_shape), F32)], left, others[0], right
    )
    known = [[(slots[n], True) for n in group] for group in groups]
    known.append([(slots[n], False) for n in groups[0]] + [(slots[last], True)])
    came = [slots[n] for n in [*groups[1], last]]
    first, normed = call(
        functools.partial(outgoing_finish_kernel, came, known), "outgoing_finish",
        [((height, side, width), F32), ((count, width), BF16)],
        others[1], *parts, part, left, gate, both, *norms, out_w, out_bias,
        scalar=me, scratch=[((height, side, hidden), F32), ((len(came), *part_shape), F32)],
    )

    pieces = gather(normed)
    others, x = [], []
    for group in groups:
        held = [slots[n] for n in group]
        outs = [((len(held), span, hidden), BF16), (x_shape, F32)]
        if not x:
            outs += [((rows * side, width), F32)]
        edge, *made = call(
            functools.partial(incoming_edges_kernel, held, side), "incoming_edges", outs,
            *[pieces[n] for n in group], *weights, *(x or [normed]),
            scalar=me, scratch=[((len(held), height * height, hidden), F32)],
        )
        if not x:
            gate = made.pop()
            others.append(flip(edge))
        x = made
    (edge,) = call(
        functools.partial(incoming_last_kernel, slots[last], side), "incoming_last",
        [((quarter, span, hidden), BF16)], pieces[last], *weights, edge, scalar=me,
    )
    others.append(flip(edge))
    x = call(
        incoming_kernel, "incoming", [(x_shape, F32)], *x, others[0], edge,
        scratch=[((quarter + 1, height * height, hidden), F32)],
    )
    (out,) = call(
        incoming_finish_kernel, "incoming_finish", [((rows, side, width), F32)],
        *x, others[1], first, gate, *norms, out_w, out_bias, scalar=me,
        scratch=[((quarter, height * height, hidden), F32), (x_shape, F32)],
    )
    return out


def solution(mesh):
    in_specs = (P(("groups", "dap"), None, None), P("groups"), P(), P(), P(), P(), P(), P())
    out_specs = P(("groups", "dap"), None, None)
    return jax.shard_map(body, mesh=mesh, in_specs=in_specs, out_specs=out_specs, check_vma=False)
```

```python
import functools

import jax
import jax.numpy as jnp
from jax import lax
from jax.experimental import pallas as pl
from jax.experimental.pallas import tpu as pltpu
from jax.sharding import PartitionSpec as P

F32 = jnp.float32
BF16 = jnp.bfloat16
VMEM = pl.BlockSpec(memory_space=pltpu.VMEM)
SMEM = pl.BlockSpec(memory_space=pltpu.SMEM)
CHUNK = 64
BLOCK = 512
PARAMS = pltpu.CompilerParams(vmem_limit_bytes=48 * 1024 * 1024)


def normalize(values, gain, shift):
    mean = jnp.mean(values, axis=-1, keepdims=True)
    centered = values - mean
    spread = jnp.mean(centered * centered, axis=-1, keepdims=True)
    return centered * lax.rsqrt(spread + 1e-05) * gain + shift


def sigmoid(values):
    return 0.5 * jnp.tanh(0.5 * values) + 0.5


def gated(normed, edge_w_ref, edge_bias_ref, layer, index, hidden):
    span = slice(index * hidden, (index + 2) * hidden)
    both = jnp.dot(normed, edge_w_ref[layer, :, span], preferred_element_type=F32)
    both = both + edge_bias_ref[layer : layer + 1, span]
    return sigmoid(both[:, :hidden]) * both[:, hidden:]


def masked(values, row, column, mask_ref):
    valid = jnp.sum(mask_ref[...].astype(F32), axis=1, keepdims=True)
    return jnp.where(jnp.maximum(row, column).astype(F32) < valid, values, 0.0)


def edges(normed_ref, out_ref, first_row, side, mask_ref, edge_w_ref, edge_bias_ref, layer, index):
    count, hidden = normed_ref.shape[0], out_ref.shape[1]
    size = min(count, BLOCK)

    def block(at):
        values = gated(
            normed_ref[pl.ds(at, size), :], edge_w_ref, edge_bias_ref, layer, index, hidden
        )
        position = at + lax.broadcasted_iota(jnp.int32, values.shape, 0)
        values = masked(values, first_row + position // side, position % side, mask_ref)
        out_ref[pl.ds(at, size), :] = values.astype(BF16).astype(out_ref.dtype)

    if count == size:
        block(0)
    else:
        pl.loop(0, count // size)(lambda n: block(pl.multiple_of(n * size, size)))


def gate_of(normed, gate_ref, edge_w_ref, edge_bias_ref, layer):
    width = gate_ref.shape[1]
    low = edge_bias_ref.shape[1] - width
    value = jnp.dot(normed, edge_w_ref[layer, :, low:], preferred_element_type=F32)
    gate_ref[...] = sigmoid(value + edge_bias_ref[layer : layer + 1, low:])


def finish(block, contracted, gate, gain_ref, shift_ref, out_w_ref, out_bias_ref, layer):
    normed = normalize(contracted, gain_ref[layer, 1:2, :], shift_ref[layer, 1:2, :]).astype(BF16)
    result = jnp.dot(normed, out_w_ref[layer], preferred_element_type=F32)
    return block + gate * (result + out_bias_ref[layer : layer + 1, :])


def chip_of(me, distances, own):
    core = me & 1 if own else 1 - (me & 1)
    near, far = distances
    return me >> 1 ^ near + (far - near) * core


def load_kernel(*refs):
    count = len(refs) // 2
    given, kept, sems = refs[:count], refs[count : 2 * count], refs[2 * count]
    copies = [
        pltpu.make_async_copy(source, target, sems.at[n])
        for n, (source, target) in enumerate(zip(given, kept))
    ]
    for copy in copies:
        copy.start()
    for copy in copies:
        copy.wait()


def norm_kernel(at_ref, pair_ref, other_ref, gain_ref, shift_ref, both_ref, normed_ref):
    rows = pair_ref.shape[0]
    core = at_ref[0] & 1
    both_ref[pl.ds(core * rows, rows)] = pair_ref[...]
    both_ref[pl.ds((1 - core) * rows, rows)] = other_ref[...]
    block = both_ref[...].reshape(normed_ref.shape)
    normed_ref[...] = normalize(block, gain_ref[0, 0:1, :], shift_ref[0, 0:1, :]).astype(BF16)


def merge(low, a, b, shift):
    return jnp.where(low, a, b) + pltpu.roll(jnp.where(low, b, a), shift, 0)


def fold(parts, sub):
    for shift in (1, 2, 4):
        low = (sub & shift) == 0
        parts = [merge(low, a, b, shift) for a, b in zip(parts[0::2], parts[1::2])]
    return parts[0]


def row_sums(left_ref, piece_ref, a, first, some, side):
    hidden = left_ref.shape[1]

    def chunk(at, totals):
        right = piece_ref[pl.ds(a * side + at, CHUNK), :].astype(F32)
        sums = []
        for i in range(first, first + some):
            product = left_ref[pl.ds(i * side + at, CHUNK), :] * right
            sums.append(jnp.sum(product.reshape(CHUNK // 8, 8, hidden), axis=0))
        return [t + s for t, s in zip(totals, sums)] if totals else sums

    totals = chunk(0, None)
    if side > CHUNK:
        totals = lax.fori_loop(
            1, side // CHUNK, lambda n, t: chunk(pl.multiple_of(n * CHUNK, CHUNK), t), totals
        )
    return totals


def products(left_ref, piece_ref, part_ref, side):
    rows, height, hidden = part_ref.shape
    sub = lax.broadcasted_iota(jnp.int32, (height, hidden), 0)
    some = 4
    for first in range(0, rows, some):
        totals = [row_sums(left_ref, piece_ref, a, first, some, side) for a in range(height)]
        for i in range(some):
            part_ref[first + i] = fold([total[i] for total in totals], sub)


def outgoing_edges_kernel(held, side, at_ref, *refs):
    normed, refs = refs[: len(held)], refs[len(held) :]
    mask_ref, edge_w_ref, edge_bias_ref, *refs = refs
    if len(refs) == 5:
        own_ref, right_ref, part_ref, left_ref, gate_ref = refs
    else:
        left_ref, right_ref, part_ref = refs
    me = at_ref[0]
    height = left_ref.shape[0] // side
    shared = (side, mask_ref, edge_w_ref, edge_bias_ref, 0)
    if len(refs) == 5:
        edges(own_ref, left_ref, (me >> 1) * height, *shared, 0)
        gate_of(own_ref[...], gate_ref, edge_w_ref, edge_bias_ref, 0)
    for n, distances in enumerate(held):
        first = chip_of(me, distances, True) * height
        edges(normed[n], right_ref.at[n], first, *shared, 2)
        products(left_ref, right_ref.at[n], part_ref.at[n], side)


def outgoing_last_kernel(
    last, side, at_ref, normed_ref, mask_ref, edge_w_ref, edge_bias_ref, right_ref
):
    height = normed_ref.shape[0] // side
    edges(
        normed_ref, right_ref.at[0], chip_of(at_ref[0], last, True) * height, side,
        mask_ref, edge_w_ref, edge_bias_ref, 0, 2,
    )


def outgoing_kernel(left_ref, *refs):
    piece_refs, part_ref = refs[:-1], refs[-1]
    side = left_ref.shape[0] // part_ref.shape[1]
    pieces = [ref.at[n] for ref in piece_refs for n in range(ref.shape[0])]
    for n, piece in enumerate(pieces):
        products(left_ref, piece, part_ref.at[n], side)


def outgoing_finish_kernel(held, given, at_ref, piece_ref, *refs):
    parts, refs = refs[: len(given)], refs[len(given) :]
    (
        left_ref, gate_ref, both_ref, gain_ref, shift_ref, out_w_ref, out_bias_ref,
        first_ref, normed_ref, x_scr, part_scr,
    ) = refs
    height, side, width = both_ref.shape
    hidden = left_ref.shape[1]
    me = at_ref[0]

    def put(part, distances, own):
        at = pl.multiple_of(chip_of(me, distances, own) * height, height)
        for i in range(height):
            x_scr[i, pl.ds(at, height), :] = part[i]

    for part, slots in zip(parts, given):
        for n, (distances, own) in enumerate(slots):
            put(part.at[n], distances, own)
    for n, distances in enumerate(held):
        products(left_ref, piece_ref.at[n], part_scr.at[n], side)
        put(part_scr.at[n], distances, False)

    block = both_ref[...].reshape(height * side, width)
    contracted = x_scr[...].reshape(height * side, hidden)
    first = finish(
        block, contracted, gate_ref[...], gain_ref, shift_ref, out_w_ref, out_bias_ref, 0
    )
    first_ref[...] = first.reshape(first_ref.shape)
    normed_ref[...] = normalize(first, gain_ref[1, 0:1, :], shift_ref[1, 0:1, :]).astype(BF16)


def add_pieces(pieces, left_scr, x_ref, start):
    rows, side, hidden = x_ref.shape
    height = 2 * rows
    for n, (piece, came) in enumerate(pieces):
        left_scr[n] = piece[height * side :, :].astype(F32)

    def columns(at):
        totals = [start(i, at) for i in range(rows)]
        for n, (piece, came) in enumerate(pieces):
            for a in range(height):
                right = piece[pl.ds(a * side + at, CHUNK), :].astype(F32)
                for i in range(rows):
                    row = a * height + came * rows + i
                    totals[i] = totals[i] + left_scr[n, row : row + 1, :] * right
        for i in range(rows):
            x_ref[i, pl.ds(at, CHUNK), :] = totals[i]

    if side == CHUNK:
        columns(0)
    else:
        pl.loop(0, side // CHUNK)(lambda n: columns(pl.multiple_of(n * CHUNK, CHUNK)))


def form_incoming(held, me, normed, out_refs, mask_ref, edge_w_ref, edge_bias_ref, side):
    chip = me >> 1
    height = normed[0].shape[0] // side
    hidden = out_refs[0].shape[1]
    columns, places = [], []
    for distances, normed_ref, out_ref in zip(held, normed, out_refs):
        first = chip_of(me, distances, True) * height
        edges(
            normed_ref, out_ref.at[pl.ds(0, height * side)], first, side,
            mask_ref, edge_w_ref, edge_bias_ref, 1, 2,
        )
        for a in range(height):
            both = normed_ref[pl.ds(pl.multiple_of(a * side + (chip >> 1) * 16, 16), 16), :]
            both = both.astype(F32)
            columns.append(jnp.where(chip & 1 == 0, both[:8], both[8:]))
            places.append(jnp.full((8, hidden), first + a, jnp.int32))
    left = gated(
        jnp.concatenate(columns, 0).astype(BF16), edge_w_ref, edge_bias_ref, 1, 0, hidden
    )
    column = chip * 8 + lax.broadcasted_iota(jnp.int32, left.shape, 0) % 8
    left = masked(left, jnp.concatenate(places, 0), column, mask_ref)
    left = left.reshape(len(held) * height, 8, hidden)
    left = jnp.where(me & 1 == 0, left, pltpu.roll(left, 4, 1))
    left = left.reshape(len(held), height * 8, hidden).astype(BF16)
    for n, out_ref in enumerate(out_refs):
        out_ref[height * side :, :] = left[n]


def incoming_edges_kernel(held, side, at_ref, *refs):
    normed, refs = refs[: len(held)], refs[len(held) :]
    mask_ref, edge_w_ref, edge_bias_ref, extra_ref, out_ref, x_ref, *refs = refs
    rows, _, hidden = x_ref.shape
    me = at_ref[0]
    if len(refs) == 2:
        gate_ref, left_scr = refs
        count = rows * side
        own = extra_ref[pl.ds(pl.multiple_of((me & 1) * count, count), count), :]
        gate_of(own, gate_ref, edge_w_ref, edge_bias_ref, 1)
        start = lambda i, at: jnp.zeros((CHUNK, hidden), F32)
    else:
        (left_scr,) = refs
        start = lambda i, at: extra_ref[i, pl.ds(at, CHUNK), :]
    outs = [out_ref.at[n] for n in range(len(held))]
    form_incoming(held, me, normed, outs, mask_ref, edge_w_ref, edge_bias_ref, side)
    add_pieces([(out, 0) for out in outs], left_scr, x_ref, start)


def incoming_last_kernel(
    last, side, at_ref, normed_ref, mask_ref, edge_w_ref, edge_bias_ref, out_ref
):
    form_incoming(
        [last], at_ref[0], [normed_ref], [out_ref.at[0]],
        mask_ref, edge_w_ref, edge_bias_ref, side,
    )


def incoming_kernel(before_ref, *refs):
    *came, last_ref, x_ref, left_scr = refs
    pieces = [(ref.at[n], 1) for ref in came for n in range(ref.shape[0])]
    pieces.append((last_ref.at[0], 0))
    add_pieces(pieces, left_scr, x_ref, lambda i, at: before_ref[i, pl.ds(at, CHUNK), :])


def incoming_finish_kernel(
    at_ref, before_ref, piece_ref, first_ref, gate_ref, gain_ref, shift_ref, out_w_ref,
    out_bias_ref, out_ref, left_scr, x_scr,
):
    rows, side, width = out_ref.shape
    hidden = gate_ref.shape[1]
    pieces = [(piece_ref.at[n], 1) for n in range(piece_ref.shape[0])]
    add_pieces(pieces, left_scr, x_scr, lambda i, at: before_ref[i, pl.ds(at, CHUNK), :])
    first = first_ref[pl.ds((at_ref[0] & 1) * rows, rows)].reshape(rows * side, width)
    out_ref[...] = finish(
        first, x_scr[...].reshape(rows * side, hidden), gate_ref[...],
        gain_ref, shift_ref, out_w_ref, out_bias_ref, 1,
    ).reshape(rows, side, width)


def call(kernel, name, outs, *operands, scalar=None, scratch=(), work=0):
    given = operands if scalar is None else (scalar, *operands)
    return pl.pallas_call(
        kernel,
        in_specs=[SMEM] * (scalar is not None) + [VMEM] * len(operands),
        out_specs=[VMEM] * len(outs),
        out_shape=[jax.ShapeDtypeStruct(*out) for out in outs],
        scratch_shapes=[pltpu.VMEM(*one) for one in scratch],
        compiler_params=PARAMS,
        cost_estimate=pl.CostEstimate(flops=work, bytes_accessed=work // 100, transcendentals=0),
        name=name,
    )(*given)


def body(pair, residue_mask, norm_gain, norm_bias, edge_w, edge_bias, out_w, out_bias):
    rows, side, width = pair.shape
    hidden = out_w.shape[1]
    dap = lax.axis_size("dap")
    chips = dap // 2
    me = lax.axis_index("dap").reshape(1)
    mask = residue_mask.reshape(1, side)
    height = 2 * rows
    count = height * side
    span = count + height * height
    half = chips // 2
    quarter = half // 2

    near = [n for n in range(half) if n % 4 in (1, 2)]
    far = [half + n for n in range(half - 2, -1, -2)]
    slots = list(zip(near, far))
    slots += [(a ^ 2, b ^ 1) for a, b in slots]
    groups = (list(range(quarter)), list(range(half - 1, quarter, -1)))
    last = quarter

    def swap(piece, distances):
        pairs = [(device, device ^ 2 * distances[device & 1]) for device in range(dap)]
        return lax.ppermute(piece, "dap", pairs)

    def flip(value):
        return lax.ppermute(value, "dap", [(device, device ^ 1) for device in range(dap)])

    def gather(own):
        pieces = [swap(own, distances) for distances in slots[:quarter]]
        return pieces + [swap(piece, (2, 1)) for piece in pieces]

    arguments = (pair, norm_gain, norm_bias, mask, edge_w, edge_bias, out_w, out_bias)
    kept = pl.pallas_call(
        load_kernel,
        in_specs=[pl.BlockSpec(memory_space=pltpu.HBM)] * len(arguments),
        out_specs=[VMEM] * len(arguments),
        out_shape=[jax.ShapeDtypeStruct(value.shape, value.dtype) for value in arguments],
        scratch_shapes=[pltpu.SemaphoreType.DMA((len(arguments),))],
        compiler_params=PARAMS,
        name="load",
    )(*[pltpu.with_memory_space_constraint(value, pltpu.HBM) for value in arguments])
    other = flip(pair)
    pair, norm_gain, norm_bias, mask, edge_w, edge_bias, out_w, out_bias = kept
    norms = (norm_gain, norm_bias)
    weights = (mask, edge_w, edge_bias)
    part_shape = (height, height, hidden)
    x_shape = (rows, side, hidden)

    both, normed = call(
        norm_kernel, "norm", [((height, side, width), F32), ((count, width), BF16)],
        pair, other, *norms, scalar=me,
    )
    pieces = gather(normed)
    others, parts = [], []
    for group in groups:
        held = [slots[n] for n in group]
        outs = [((len(held), count, hidden), BF16), ((len(held), *part_shape), F32)]
        if not parts:
            outs += [((count, hidden), F32), ((count, width), F32)]
        right, part, *rest = call(
            functools.partial(outgoing_edges_kernel, held, side), "outgoing_edges", outs,
            *[pieces[n] for n in group], *weights, left if parts else normed, scalar=me,
        )
        if rest:
            left, gate = rest
        others.append(flip(right))
        parts.append(part)
    (right,) = call(
        functools.partial(outgoing_last_kernel, slots[last], side), "outgoing_last",
        [((1, count, hidden), BF16)], pieces[last], *weights, scalar=me, work=10**10,
    )
    others.append(flip(right))
    (part,) = call(
        outgoing_kernel, "outgoing", [((half, *part_shape), F32)], left, *others[:2], right
    )
    known = [[(slots[n], True) for n in group] for group in groups]
    known.append([(slots[n], False) for n in groups[0] + groups[1]] + [(slots[last], True)])
    came = [slots[last]]
    first, normed = call(
        functools.partial(outgoing_finish_kernel, came, known), "outgoing_finish",
        [((height, side, width), F32), ((count, width), BF16)],
        others[2], *parts, part, left, gate, both, *norms, out_w, out_bias,
        scalar=me, scratch=[((height, side, hidden), F32), ((len(came), *part_shape), F32)],
    )

    pieces = gather(normed)
    others, x = [], []
    for group in groups:
        held = [slots[n] for n in group]
        outs = [((len(held), span, hidden), BF16), (x_shape, F32)]
        if not x:
            outs += [((rows * side, width), F32)]
        edge, *made = call(
            functools.partial(incoming_edges_kernel, held, side), "incoming_edges", outs,
            *[pieces[n] for n in group], *weights, *(x or [normed]),
            scalar=me, scratch=[((len(held), height * height, hidden), F32)],
        )
        if not x:
            gate = made.pop()
        others.append(flip(edge))
        x = made
    (edge,) = call(
        functools.partial(incoming_last_kernel, slots[last], side), "incoming_last",
        [((1, span, hidden), BF16)], pieces[last], *weights, scalar=me, work=10**10,
    )
    others.append(flip(edge))
    x = call(
        incoming_kernel, "incoming", [(x_shape, F32)], *x, *others[:2], edge,
        scratch=[((half, height * height, hidden), F32)],
    )
    (out,) = call(
        incoming_finish_kernel, "incoming_finish", [((rows, side, width), F32)],
        *x, others[2], first, gate, *norms, out_w, out_bias, scalar=me,
        scratch=[((1, height * height, hidden), F32), (x_shape, F32)],
    )
    return out


def solution(mesh):
    in_specs = (P(("groups", "dap"), None, None), P("groups"), P(), P(), P(), P(), P(), P())
    out_specs = P(("groups", "dap"), None, None)
    return jax.shard_map(body, mesh=mesh, in_specs=in_specs, out_specs=out_specs, check_vma=False)
```

```python
import functools

import jax
import jax.numpy as jnp
from jax import lax
from jax.experimental import pallas as pl
from jax.experimental.pallas import tpu as pltpu
from jax.sharding import PartitionSpec as P

F32 = jnp.float32
BF16 = jnp.bfloat16
VMEM = pl.BlockSpec(memory_space=pltpu.VMEM)
SMEM = pl.BlockSpec(memory_space=pltpu.SMEM)
CHUNK = 64
BLOCK = 512
PARAMS = pltpu.CompilerParams(vmem_limit_bytes=48 * 1024 * 1024)


def normalize(values, gain, shift):
    scale = 1.0 / values.shape[-1]
    mean = jnp.sum(values, axis=-1, keepdims=True) * scale
    centered = values - mean
    spread = jnp.sum(centered * centered, axis=-1, keepdims=True) * scale
    return centered * lax.rsqrt(spread + 1e-05) * gain + shift


def sigmoid(values):
    return 0.5 * jnp.tanh(0.5 * values) + 0.5


def gated(normed, edge_w_ref, edge_bias_ref, layer, index, hidden):
    span = slice(index * hidden, (index + 2) * hidden)
    both = jnp.dot(normed, edge_w_ref[layer, :, span], preferred_element_type=F32)
    both = both + edge_bias_ref[layer : layer + 1, span]
    return sigmoid(both[:, :hidden]) * both[:, hidden:]


def masked(values, row, column, mask_ref):
    valid = jnp.sum(mask_ref[...].astype(F32), axis=1, keepdims=True)
    return jnp.where(jnp.maximum(row, column).astype(F32) < valid, values, 0.0)


def edges(normed_ref, out_ref, first_row, side, mask_ref, edge_w_ref, edge_bias_ref, layer, index):
    count, hidden = normed_ref.shape[0], out_ref.shape[1]
    size = min(count, max(BLOCK, side))

    def block(at):
        values = gated(
            normed_ref[pl.ds(at, size), :], edge_w_ref, edge_bias_ref, layer, index, hidden
        )
        grid = (size // side, side, hidden)
        row = lax.broadcasted_iota(jnp.int32, grid, 0).reshape(values.shape)
        column = lax.broadcasted_iota(jnp.int32, grid, 1).reshape(values.shape)
        values = masked(values, first_row + at // side + row, column, mask_ref)
        out_ref[pl.ds(at, size), :] = values.astype(BF16).astype(out_ref.dtype)

    if count == size:
        block(0)
    else:
        pl.loop(0, count // size)(lambda n: block(pl.multiple_of(n * size, size)))


def gate_of(normed, gate_ref, edge_w_ref, edge_bias_ref, layer):
    width = gate_ref.shape[1]
    low = edge_bias_ref.shape[1] - width
    value = jnp.dot(normed, edge_w_ref[layer, :, low:], preferred_element_type=F32)
    gate_ref[...] = sigmoid(value + edge_bias_ref[layer : layer + 1, low:])


def finish(block, contracted, gate, gain_ref, shift_ref, out_w_ref, out_bias_ref, layer):
    normed = normalize(contracted, gain_ref[layer, 1:2, :], shift_ref[layer, 1:2, :]).astype(BF16)
    result = jnp.dot(normed, out_w_ref[layer], preferred_element_type=F32)
    return block + gate * (result + out_bias_ref[layer : layer + 1, :])


def chip_of(me, distances, own):
    core = me & 1 if own else 1 - (me & 1)
    near, far = distances
    return me >> 1 ^ near + (far - near) * core


def load_kernel(*refs):
    count = len(refs) // 2 - 1
    given, kept, (normed_ref, sems) = refs[:count], refs[count : 2 * count], refs[2 * count :]
    copies = [
        pltpu.make_async_copy(source, target, sems.at[n])
        for n, (source, target) in enumerate(zip(given, kept))
    ]
    for copy in copies:
        copy.start()
    for copy in copies[:3]:
        copy.wait()
    first_normed(*kept[:3], normed_ref)
    for copy in copies[3:]:
        copy.wait()


def first_normed(pair_ref, gain_ref, shift_ref, normed_ref):
    block = pair_ref[...].reshape(normed_ref.shape)
    normed_ref[...] = normalize(block, gain_ref[0, 0:1, :], shift_ref[0, 0:1, :]).astype(BF16)


def norm_kernel(
    at_ref, pair_ref, own_ref, other_ref, gain_ref, shift_ref, both_ref, normed_ref
):
    rows, side, _ = pair_ref.shape
    count = rows * side
    core = at_ref[0] & 1
    both_ref[pl.ds(core * rows, rows)] = pair_ref[...]
    both_ref[pl.ds((1 - core) * rows, rows)] = other_ref[...]
    normed_ref[pl.ds(pl.multiple_of(core * count, count), count), :] = own_ref[...]
    part = normed_ref.at[pl.ds(pl.multiple_of((1 - core) * count, count), count)]
    first_normed(other_ref, gain_ref, shift_ref, part)


def merge(low, a, b, shift):
    return jnp.where(low, a, b) + pltpu.roll(jnp.where(low, b, a), shift, 0)


def fold(parts, sub):
    for shift in (1, 2, 4):
        low = (sub & shift) == 0
        parts = [merge(low, a, b, shift) for a, b in zip(parts[0::2], parts[1::2])]
    return parts[0]


def row_sums(left_ref, piece_ref, a, first, some, side):
    hidden = left_ref.shape[1]

    def chunk(at, totals):
        right = piece_ref[pl.ds(a * side + at, CHUNK), :].astype(F32)
        sums = []
        for i in range(first, first + some):
            product = left_ref[pl.ds(i * side + at, CHUNK), :] * right
            sums.append(jnp.sum(product.reshape(CHUNK // 8, 8, hidden), axis=0))
        return [t + s for t, s in zip(totals, sums)] if totals else sums

    totals = chunk(0, None)
    if side > CHUNK:
        totals = lax.fori_loop(
            1, side // CHUNK, lambda n, t: chunk(pl.multiple_of(n * CHUNK, CHUNK), t), totals
        )
    return totals


def products(left_ref, piece_ref, part_ref, side):
    rows, height, hidden = part_ref.shape
    sub = lax.broadcasted_iota(jnp.int32, (height, hidden), 0)
    some = 4
    for first in range(0, rows, some):
        totals = [row_sums(left_ref, piece_ref, a, first, some, side) for a in range(height)]
        for i in range(some):
            part_ref[first + i] = fold([total[i] for total in totals], sub)


def outgoing_edges_kernel(held, side, at_ref, *refs):
    normed, refs = refs[: len(held)], refs[len(held) :]
    mask_ref, edge_w_ref, edge_bias_ref, *refs = refs
    if len(refs) == 5:
        own_ref, right_ref, part_ref, left_ref, gate_ref = refs
    else:
        left_ref, right_ref, part_ref = refs
    me = at_ref[0]
    height = left_ref.shape[0] // side
    shared = (side, mask_ref, edge_w_ref, edge_bias_ref, 0)
    if len(refs) == 5:
        edges(own_ref, left_ref, (me >> 1) * height, *shared, 0)
        gate_of(own_ref[...], gate_ref, edge_w_ref, edge_bias_ref, 0)
    for n, distances in enumerate(held):
        first = chip_of(me, distances, True) * height
        edges(normed[n], right_ref.at[n], first, *shared, 2)
        products(left_ref, right_ref.at[n], part_ref.at[n], side)


def outgoing_last_kernel(
    last, side, at_ref, normed_ref, mask_ref, edge_w_ref, edge_bias_ref, right_ref
):
    height = normed_ref.shape[0] // side
    edges(
        normed_ref, right_ref.at[0], chip_of(at_ref[0], last, True) * height, side,
        mask_ref, edge_w_ref, edge_bias_ref, 0, 2,
    )


def outgoing_kernel(left_ref, *refs):
    piece_refs, part_ref = refs[:-1], refs[-1]
    side = left_ref.shape[0] // part_ref.shape[1]
    pieces = [ref.at[n] for ref in piece_refs for n in range(ref.shape[0])]
    for n, piece in enumerate(pieces):
        products(left_ref, piece, part_ref.at[n], side)


def outgoing_finish_kernel(held, given, at_ref, piece_ref, *refs):
    parts, refs = refs[: len(given)], refs[len(given) :]
    (
        left_ref, gate_ref, both_ref, gain_ref, shift_ref, out_w_ref, out_bias_ref,
        first_ref, normed_ref, x_scr, part_scr,
    ) = refs
    height, side, width = both_ref.shape
    hidden = left_ref.shape[1]
    me = at_ref[0]

    def put(part, distances, own):
        at = pl.multiple_of(chip_of(me, distances, own) * height, height)
        for i in range(height):
            x_scr[i, pl.ds(at, height), :] = part[i]

    for part, slots in zip(parts, given):
        for n, (distances, own) in enumerate(slots):
            put(part.at[n], distances, own)
    for n, distances in enumerate(held):
        products(left_ref, piece_ref.at[n], part_scr.at[n], side)
        put(part_scr.at[n], distances, False)

    block = both_ref[...].reshape(height * side, width)
    contracted = x_scr[...].reshape(height * side, hidden)
    first = finish(
        block, contracted, gate_ref[...], gain_ref, shift_ref, out_w_ref, out_bias_ref, 0
    )
    first_ref[...] = first.reshape(first_ref.shape)
    normed_ref[...] = normalize(first, gain_ref[1, 0:1, :], shift_ref[1, 0:1, :]).astype(BF16)


def add_pieces(pieces, left_scr, x_ref, start):
    rows, side, hidden = x_ref.shape
    height = 2 * rows
    for n, (piece, came) in enumerate(pieces):
        left_scr[n] = piece[height * side :, :].astype(F32)

    def columns(at):
        totals = [start(i, at) for i in range(rows)]
        for n, (piece, came) in enumerate(pieces):
            for a in range(height):
                right = piece[pl.ds(a * side + at, CHUNK), :].astype(F32)
                for i in range(rows):
                    row = a * height + came * rows + i
                    totals[i] = totals[i] + left_scr[n, row : row + 1, :] * right
        for i in range(rows):
            x_ref[i, pl.ds(at, CHUNK), :] = totals[i]

    if side == CHUNK:
        columns(0)
    else:
        pl.loop(0, side // CHUNK)(lambda n: columns(pl.multiple_of(n * CHUNK, CHUNK)))


def form_incoming(held, me, normed, out_refs, mask_ref, edge_w_ref, edge_bias_ref, side):
    chip = me >> 1
    height = normed[0].shape[0] // side
    hidden = out_refs[0].shape[1]
    columns, places = [], []
    for distances, normed_ref, out_ref in zip(held, normed, out_refs):
        first = chip_of(me, distances, True) * height
        edges(
            normed_ref, out_ref.at[pl.ds(0, height * side)], first, side,
            mask_ref, edge_w_ref, edge_bias_ref, 1, 2,
        )
        for a in range(height):
            both = normed_ref[pl.ds(pl.multiple_of(a * side + (chip >> 1) * 16, 16), 16), :]
            both = both.astype(F32)
            columns.append(jnp.where(chip & 1 == 0, both[:8], both[8:]))
            places.append(jnp.full((8, hidden), first + a, jnp.int32))
    left = gated(
        jnp.concatenate(columns, 0).astype(BF16), edge_w_ref, edge_bias_ref, 1, 0, hidden
    )
    column = chip * 8 + lax.broadcasted_iota(jnp.int32, left.shape, 0) % 8
    left = masked(left, jnp.concatenate(places, 0), column, mask_ref)
    left = left.reshape(len(held) * height, 8, hidden)
    left = jnp.where(me & 1 == 0, left, pltpu.roll(left, 4, 1))
    left = left.reshape(len(held), height * 8, hidden).astype(BF16)
    for n, out_ref in enumerate(out_refs):
        out_ref[height * side :, :] = left[n]


def incoming_edges_kernel(held, side, at_ref, *refs):
    normed, refs = refs[: len(held)], refs[len(held) :]
    mask_ref, edge_w_ref, edge_bias_ref, extra_ref, out_ref, x_ref, *refs = refs
    rows, _, hidden = x_ref.shape
    me = at_ref[0]
    if len(refs) == 2:
        gate_ref, left_scr = refs
        count = rows * side
        own = extra_ref[pl.ds(pl.multiple_of((me & 1) * count, count), count), :]
        gate_of(own, gate_ref, edge_w_ref, edge_bias_ref, 1)
        start = lambda i, at: jnp.zeros((CHUNK, hidden), F32)
    else:
        (left_scr,) = refs
        start = lambda i, at: extra_ref[i, pl.ds(at, CHUNK), :]
    outs = [out_ref.at[n] for n in range(len(held))]
    form_incoming(held, me, normed, outs, mask_ref, edge_w_ref, edge_bias_ref, side)
    add_pieces([(out, 0) for out in outs], left_scr, x_ref, start)


def incoming_last_kernel(
    last, side, at_ref, normed_ref, mask_ref, edge_w_ref, edge_bias_ref, out_ref
):
    form_incoming(
        [last], at_ref[0], [normed_ref], [out_ref.at[0]],
        mask_ref, edge_w_ref, edge_bias_ref, side,
    )


def incoming_kernel(before_ref, *refs):
    *came, last_ref, x_ref, left_scr = refs
    pieces = [(ref.at[n], 1) for ref in came for n in range(ref.shape[0])]
    pieces.append((last_ref.at[0], 0))
    add_pieces(pieces, left_scr, x_ref, lambda i, at: before_ref[i, pl.ds(at, CHUNK), :])


def incoming_finish_kernel(
    at_ref, before_ref, piece_ref, first_ref, gate_ref, gain_ref, shift_ref, out_w_ref,
    out_bias_ref, out_ref, left_scr, x_scr,
):
    rows, side, width = out_ref.shape
    hidden = gate_ref.shape[1]
    pieces = [(piece_ref.at[n], 1) for n in range(piece_ref.shape[0])]
    add_pieces(pieces, left_scr, x_scr, lambda i, at: before_ref[i, pl.ds(at, CHUNK), :])
    first = first_ref[pl.ds((at_ref[0] & 1) * rows, rows)].reshape(rows * side, width)
    out_ref[...] = finish(
        first, x_scr[...].reshape(rows * side, hidden), gate_ref[...],
        gain_ref, shift_ref, out_w_ref, out_bias_ref, 1,
    ).reshape(rows, side, width)


def call(kernel, name, outs, *operands, scalar=None, scratch=(), work=0):
    given = operands if scalar is None else (scalar, *operands)
    return pl.pallas_call(
        kernel,
        in_specs=[SMEM] * (scalar is not None) + [VMEM] * len(operands),
        out_specs=[VMEM] * len(outs),
        out_shape=[jax.ShapeDtypeStruct(*out) for out in outs],
        scratch_shapes=[pltpu.VMEM(*one) for one in scratch],
        compiler_params=PARAMS,
        cost_estimate=pl.CostEstimate(flops=work, bytes_accessed=work // 100, transcendentals=0),
        name=name,
    )(*given)


def body(pair, residue_mask, norm_gain, norm_bias, edge_w, edge_bias, out_w, out_bias):
    rows, side, width = pair.shape
    hidden = out_w.shape[1]
    dap = lax.axis_size("dap")
    chips = dap // 2
    me = lax.axis_index("dap").reshape(1)
    mask = residue_mask.reshape(1, side)
    height = 2 * rows
    count = height * side
    span = count + height * height
    half = chips // 2
    quarter = half // 2

    near = [n for n in range(half) if n % 4 in (1, 2)]
    far = [half + n for n in range(half - 2, -1, -2)]
    slots = list(zip(near, far))
    slots += [(a ^ 2, b ^ 1) for a, b in slots]
    groups = (list(range(quarter)), list(range(half - 1, quarter, -1)))
    last = quarter

    def swap(piece, distances):
        pairs = [(device, device ^ 2 * distances[device & 1]) for device in range(dap)]
        return lax.ppermute(piece, "dap", pairs)

    def flip(value):
        return lax.ppermute(value, "dap", [(device, device ^ 1) for device in range(dap)])

    def gather(own):
        pieces = [swap(own, distances) for distances in slots[:quarter]]
        return pieces + [swap(piece, (2, 1)) for piece in pieces]

    arguments = (pair, norm_gain, norm_bias, mask, edge_w, edge_bias, out_w, out_bias)
    *kept, normed = pl.pallas_call(
        load_kernel,
        in_specs=[pl.BlockSpec(memory_space=pltpu.HBM)] * len(arguments),
        out_specs=[VMEM] * (len(arguments) + 1),
        out_shape=[jax.ShapeDtypeStruct(value.shape, value.dtype) for value in arguments]
        + [jax.ShapeDtypeStruct((rows * side, width), BF16)],
        scratch_shapes=[pltpu.SemaphoreType.DMA((len(arguments),))],
        compiler_params=PARAMS,
        name="load",
    )(*[pltpu.with_memory_space_constraint(value, pltpu.HBM) for value in arguments])
    other = flip(pair)
    pair, norm_gain, norm_bias, mask, edge_w, edge_bias, out_w, out_bias = kept
    norms = (norm_gain, norm_bias)
    weights = (mask, edge_w, edge_bias)
    part_shape = (height, height, hidden)
    x_shape = (rows, side, hidden)

    both, normed = call(
        norm_kernel, "norm", [((height, side, width), F32), ((count, width), BF16)],
        pair, normed, other, *norms, scalar=me,
    )
    pieces = gather(normed)
    others, parts = [], []
    for group in groups:
        held = [slots[n] for n in group]
        outs = [((len(held), count, hidden), BF16), ((len(held), *part_shape), F32)]
        if not parts:
            outs += [((count, hidden), F32), ((count, width), F32)]
        right, part, *rest = call(
            functools.partial(outgoing_edges_kernel, held, side), "outgoing_edges", outs,
            *[pieces[n] for n in group], *weights, left if parts else normed, scalar=me,
        )
        if rest:
            left, gate = rest
        others.append(flip(right))
        parts.append(part)
    (right,) = call(
        functools.partial(outgoing_last_kernel, slots[last], side), "outgoing_last",
        [((1, count, hidden), BF16)], pieces[last], *weights, scalar=me, work=10**10,
    )
    others.append(flip(right))
    (part,) = call(
        outgoing_kernel, "outgoing", [((half, *part_shape), F32)], left, *others[:2], right
    )
    known = [[(slots[n], True) for n in group] for group in groups]
    known.append([(slots[n], False) for n in groups[0] + groups[1]] + [(slots[last], True)])
    came = [slots[last]]
    first, normed = call(
        functools.partial(outgoing_finish_kernel, came, known), "outgoing_finish",
        [((height, side, width), F32), ((count, width), BF16)],
        others[2], *parts, part, left, gate, both, *norms, out_w, out_bias,
        scalar=me, scratch=[((height, side, hidden), F32), ((len(came), *part_shape), F32)],
    )

    pieces = gather(normed)
    others, x = [], []
    for group in groups:
        held = [slots[n] for n in group]
        outs = [((len(held), span, hidden), BF16), (x_shape, F32)]
        if not x:
            outs += [((rows * side, width), F32)]
        edge, *made = call(
            functools.partial(incoming_edges_kernel, held, side), "incoming_edges", outs,
            *[pieces[n] for n in group], *weights, *(x or [normed]),
            scalar=me, scratch=[((len(held), height * height, hidden), F32)],
        )
        if not x:
            gate = made.pop()
        others.append(flip(edge))
        x = made
    (edge,) = call(
        functools.partial(incoming_last_kernel, slots[last], side), "incoming_last",
        [((1, span, hidden), BF16)], pieces[last], *weights, scalar=me, work=10**10,
    )
    others.append(flip(edge))
    x = call(
        incoming_kernel, "incoming", [(x_shape, F32)], *x, *others[:2], edge,
        scratch=[((half, height * height, hidden), F32)],
    )
    (out,) = call(
        incoming_finish_kernel, "incoming_finish", [((rows, side, width), F32)],
        *x, others[2], first, gate, *norms, out_w, out_bias, scalar=me,
        scratch=[((1, height * height, hidden), F32), (x_shape, F32)],
    )
    return out


def solution(mesh):
    in_specs = (P(("groups", "dap"), None, None), P("groups"), P(), P(), P(), P(), P(), P())
    out_specs = P(("groups", "dap"), None, None)
    return jax.shard_map(body, mesh=mesh, in_specs=in_specs, out_specs=out_specs, check_vma=False)
```

```python
import functools

import jax
import jax.numpy as jnp
from jax import lax
from jax.experimental import pallas as pl
from jax.experimental.pallas import tpu as pltpu
from jax.sharding import PartitionSpec as P

F32 = jnp.float32
BF16 = jnp.bfloat16
VMEM = pl.BlockSpec(memory_space=pltpu.VMEM)
SMEM = pl.BlockSpec(memory_space=pltpu.SMEM)
CHUNK = 64
BLOCK = 512
PARAMS = pltpu.CompilerParams(vmem_limit_bytes=48 * 1024 * 1024)


def normalize(values, gain, shift):
    scale = 1.0 / values.shape[-1]
    mean = jnp.sum(values, axis=-1, keepdims=True) * scale
    centered = values - mean
    spread = jnp.sum(centered * centered, axis=-1, keepdims=True) * scale
    return centered * lax.rsqrt(spread + 1e-05) * gain + shift


def sigmoid(values):
    return 0.5 * jnp.tanh(0.5 * values) + 0.5


def gated(normed, edge_w_ref, edge_bias_ref, layer, index, hidden):
    span = slice(index * hidden, (index + 2) * hidden)
    both = jnp.dot(normed, edge_w_ref[layer, :, span], preferred_element_type=F32)
    both = both + edge_bias_ref[layer : layer + 1, span]
    return sigmoid(both[:, :hidden]) * both[:, hidden:]


def masked(values, row, column, mask_ref):
    valid = jnp.sum(mask_ref[...].astype(F32), axis=1, keepdims=True)
    return jnp.where(jnp.maximum(row, column).astype(F32) < valid, values, 0.0)


def edges(normed_ref, out_ref, first_row, side, mask_ref, edge_w_ref, edge_bias_ref, layer, index):
    count, hidden = normed_ref.shape[0], out_ref.shape[1]
    size = min(count, max(BLOCK, side))

    def block(at):
        values = gated(
            normed_ref[pl.ds(at, size), :], edge_w_ref, edge_bias_ref, layer, index, hidden
        )
        grid = (size // side, side, hidden)
        row = lax.broadcasted_iota(jnp.int32, grid, 0).reshape(values.shape)
        column = lax.broadcasted_iota(jnp.int32, grid, 1).reshape(values.shape)
        values = masked(values, first_row + at // side + row, column, mask_ref)
        out_ref[pl.ds(at, size), :] = values.astype(BF16).astype(out_ref.dtype)

    if count == size:
        block(0)
    else:
        pl.loop(0, count // size)(lambda n: block(pl.multiple_of(n * size, size)))


def gate_of(normed, gate_ref, edge_w_ref, edge_bias_ref, layer):
    width = gate_ref.shape[1]
    low = edge_bias_ref.shape[1] - width
    value = jnp.dot(normed, edge_w_ref[layer, :, low:], preferred_element_type=F32)
    gate_ref[...] = sigmoid(value + edge_bias_ref[layer : layer + 1, low:])


def finish(block, contracted, gate, gain_ref, shift_ref, out_w_ref, out_bias_ref, layer):
    normed = normalize(contracted, gain_ref[layer, 1:2, :], shift_ref[layer, 1:2, :]).astype(BF16)
    result = jnp.dot(normed, out_w_ref[layer], preferred_element_type=F32)
    return block + gate * (result + out_bias_ref[layer : layer + 1, :])


def chip_of(me, distances, own):
    core = me & 1 if own else 1 - (me & 1)
    near, far = distances
    return me >> 1 ^ near + (far - near) * core


def load_kernel(*refs):
    count = len(refs) // 2 - 1
    given, kept, (normed_ref, sems) = refs[:count], refs[count : 2 * count], refs[2 * count :]
    copies = [
        pltpu.make_async_copy(source, target, sems.at[n])
        for n, (source, target) in enumerate(zip(given, kept))
    ]
    for copy in copies:
        copy.start()
    for copy in copies[:3]:
        copy.wait()
    first_normed(*kept[:3], normed_ref)
    for copy in copies[3:]:
        copy.wait()


def first_normed(pair_ref, gain_ref, shift_ref, normed_ref):
    block = pair_ref[...].reshape(normed_ref.shape)
    normed_ref[...] = normalize(block, gain_ref[0, 0:1, :], shift_ref[0, 0:1, :]).astype(BF16)


def norm_kernel(
    at_ref, pair_ref, own_ref, other_ref, gain_ref, shift_ref, both_ref, normed_ref
):
    rows, side, _ = pair_ref.shape
    count = rows * side
    core = at_ref[0] & 1
    both_ref[pl.ds(core * rows, rows)] = pair_ref[...]
    both_ref[pl.ds((1 - core) * rows, rows)] = other_ref[...]
    normed_ref[pl.ds(pl.multiple_of(core * count, count), count), :] = own_ref[...]
    part = normed_ref.at[pl.ds(pl.multiple_of((1 - core) * count, count), count)]
    first_normed(other_ref, gain_ref, shift_ref, part)


def merge(low, a, b, shift):
    return jnp.where(low, a, b) + pltpu.roll(jnp.where(low, b, a), shift, 0)


def fold(parts, sub):
    for shift in (1, 2, 4):
        low = (sub & shift) == 0
        parts = [merge(low, a, b, shift) for a, b in zip(parts[0::2], parts[1::2])]
    return parts[0]


def row_sums(left_ref, piece_ref, a, first, some, side):
    hidden = left_ref.shape[1]

    def chunk(at, totals):
        right = piece_ref[pl.ds(a * side + at, CHUNK), :].astype(F32)
        sums = []
        for i in range(first, first + some):
            product = left_ref[pl.ds(i * side + at, CHUNK), :] * right
            sums.append(jnp.sum(product.reshape(CHUNK // 8, 8, hidden), axis=0))
        return [t + s for t, s in zip(totals, sums)] if totals else sums

    totals = chunk(0, None)
    if side > CHUNK:
        totals = lax.fori_loop(
            1, side // CHUNK, lambda n, t: chunk(pl.multiple_of(n * CHUNK, CHUNK), t), totals
        )
    return totals


def products(left_ref, piece_ref, part_ref, side):
    rows, height, hidden = part_ref.shape
    sub = lax.broadcasted_iota(jnp.int32, (height, hidden), 0)
    some = 8
    for first in range(0, rows, some):
        totals = [row_sums(left_ref, piece_ref, a, first, some, side) for a in range(height)]
        for i in range(some):
            part_ref[first + i] = fold([total[i] for total in totals], sub)


def outgoing_edges_kernel(held, side, at_ref, *refs):
    normed, refs = refs[: len(held)], refs[len(held) :]
    mask_ref, edge_w_ref, edge_bias_ref, *refs = refs
    if len(refs) == 5:
        own_ref, right_ref, part_ref, left_ref, gate_ref = refs
    else:
        left_ref, right_ref, part_ref = refs
    me = at_ref[0]
    height = left_ref.shape[0] // side
    shared = (side, mask_ref, edge_w_ref, edge_bias_ref, 0)
    if len(refs) == 5:
        edges(own_ref, left_ref, (me >> 1) * height, *shared, 0)
        gate_of(own_ref[...], gate_ref, edge_w_ref, edge_bias_ref, 0)
    for n, distances in enumerate(held):
        first = chip_of(me, distances, True) * height
        edges(normed[n], right_ref.at[n], first, *shared, 2)
        products(left_ref, right_ref.at[n], part_ref.at[n], side)


def outgoing_last_kernel(
    last, side, at_ref, normed_ref, mask_ref, edge_w_ref, edge_bias_ref, right_ref
):
    height = normed_ref.shape[0] // side
    edges(
        normed_ref, right_ref.at[0], chip_of(at_ref[0], last, True) * height, side,
        mask_ref, edge_w_ref, edge_bias_ref, 0, 2,
    )


def outgoing_kernel(left_ref, *refs):
    piece_refs, part_ref = refs[:-1], refs[-1]
    side = left_ref.shape[0] // part_ref.shape[1]
    pieces = [ref.at[n] for ref in piece_refs for n in range(ref.shape[0])]
    for n, piece in enumerate(pieces):
        products(left_ref, piece, part_ref.at[n], side)


def outgoing_finish_kernel(held, given, at_ref, piece_ref, *refs):
    parts, refs = refs[: len(given)], refs[len(given) :]
    (
        left_ref, gate_ref, both_ref, gain_ref, shift_ref, out_w_ref, out_bias_ref,
        first_ref, normed_ref, x_scr, part_scr,
    ) = refs
    height, side, width = both_ref.shape
    hidden = left_ref.shape[1]
    me = at_ref[0]

    def put(part, distances, own):
        at = pl.multiple_of(chip_of(me, distances, own) * height, height)
        for i in range(height):
            x_scr[i, pl.ds(at, height), :] = part[i]

    for part, slots in zip(parts, given):
        for n, (distances, own) in enumerate(slots):
            put(part.at[n], distances, own)
    for n, distances in enumerate(held):
        products(left_ref, piece_ref.at[n], part_scr.at[n], side)
        put(part_scr.at[n], distances, False)

    block = both_ref[...].reshape(height * side, width)
    contracted = x_scr[...].reshape(height * side, hidden)
    first = finish(
        block, contracted, gate_ref[...], gain_ref, shift_ref, out_w_ref, out_bias_ref, 0
    )
    first_ref[...] = first.reshape(first_ref.shape)
    normed_ref[...] = normalize(first, gain_ref[1, 0:1, :], shift_ref[1, 0:1, :]).astype(BF16)


def add_pieces(pieces, left_scr, x_ref, start):
    rows, side, hidden = x_ref.shape
    height = 2 * rows
    for n, (piece, came) in enumerate(pieces):
        left_scr[n] = piece[height * side :, :].astype(F32)

    def columns(at):
        totals = [start(i, at) for i in range(rows)]
        for n, (piece, came) in enumerate(pieces):
            for a in range(height):
                right = piece[pl.ds(a * side + at, CHUNK), :].astype(F32)
                for i in range(rows):
                    row = a * height + came * rows + i
                    totals[i] = totals[i] + left_scr[n, row : row + 1, :] * right
        for i in range(rows):
            x_ref[i, pl.ds(at, CHUNK), :] = totals[i]

    if side == CHUNK:
        columns(0)
    else:
        pl.loop(0, side // CHUNK)(lambda n: columns(pl.multiple_of(n * CHUNK, CHUNK)))


def form_incoming(held, me, normed, out_refs, mask_ref, edge_w_ref, edge_bias_ref, side):
    chip = me >> 1
    height = normed[0].shape[0] // side
    hidden = out_refs[0].shape[1]
    columns, places = [], []
    for distances, normed_ref, out_ref in zip(held, normed, out_refs):
        first = chip_of(me, distances, True) * height
        edges(
            normed_ref, out_ref.at[pl.ds(0, height * side)], first, side,
            mask_ref, edge_w_ref, edge_bias_ref, 1, 2,
        )
        for a in range(height):
            both = normed_ref[pl.ds(pl.multiple_of(a * side + (chip >> 1) * 16, 16), 16), :]
            both = both.astype(F32)
            columns.append(jnp.where(chip & 1 == 0, both[:8], both[8:]))
            places.append(jnp.full((8, hidden), first + a, jnp.int32))
    left = gated(
        jnp.concatenate(columns, 0).astype(BF16), edge_w_ref, edge_bias_ref, 1, 0, hidden
    )
    column = chip * 8 + lax.broadcasted_iota(jnp.int32, left.shape, 0) % 8
    left = masked(left, jnp.concatenate(places, 0), column, mask_ref)
    left = left.reshape(len(held) * height, 8, hidden)
    left = jnp.where(me & 1 == 0, left, pltpu.roll(left, 4, 1))
    left = left.reshape(len(held), height * 8, hidden).astype(BF16)
    for n, out_ref in enumerate(out_refs):
        out_ref[height * side :, :] = left[n]


def incoming_edges_kernel(held, side, at_ref, *refs):
    normed, refs = refs[: len(held)], refs[len(held) :]
    mask_ref, edge_w_ref, edge_bias_ref, extra_ref, out_ref, x_ref, *refs = refs
    rows, _, hidden = x_ref.shape
    me = at_ref[0]
    if len(refs) == 2:
        gate_ref, left_scr = refs
        count = rows * side
        own = extra_ref[pl.ds(pl.multiple_of((me & 1) * count, count), count), :]
        gate_of(own, gate_ref, edge_w_ref, edge_bias_ref, 1)
        start = lambda i, at: jnp.zeros((CHUNK, hidden), F32)
    else:
        (left_scr,) = refs
        start = lambda i, at: extra_ref[i, pl.ds(at, CHUNK), :]
    outs = [out_ref.at[n] for n in range(len(held))]
    form_incoming(held, me, normed, outs, mask_ref, edge_w_ref, edge_bias_ref, side)
    add_pieces([(out, 0) for out in outs], left_scr, x_ref, start)


def incoming_last_kernel(
    last, side, at_ref, normed_ref, mask_ref, edge_w_ref, edge_bias_ref, out_ref
):
    form_incoming(
        [last], at_ref[0], [normed_ref], [out_ref.at[0]],
        mask_ref, edge_w_ref, edge_bias_ref, side,
    )


def incoming_kernel(before_ref, *refs):
    *came, last_ref, x_ref, left_scr = refs
    pieces = [(ref.at[n], 1) for ref in came for n in range(ref.shape[0])]
    pieces.append((last_ref.at[0], 0))
    add_pieces(pieces, left_scr, x_ref, lambda i, at: before_ref[i, pl.ds(at, CHUNK), :])


def incoming_finish_kernel(
    at_ref, before_ref, piece_ref, first_ref, gate_ref, gain_ref, shift_ref, out_w_ref,
    out_bias_ref, out_ref, left_scr, x_scr,
):
    rows, side, width = out_ref.shape
    hidden = gate_ref.shape[1]
    pieces = [(piece_ref.at[n], 1) for n in range(piece_ref.shape[0])]
    add_pieces(pieces, left_scr, x_scr, lambda i, at: before_ref[i, pl.ds(at, CHUNK), :])
    first = first_ref[pl.ds((at_ref[0] & 1) * rows, rows)].reshape(rows * side, width)
    out_ref[...] = finish(
        first, x_scr[...].reshape(rows * side, hidden), gate_ref[...],
        gain_ref, shift_ref, out_w_ref, out_bias_ref, 1,
    ).reshape(rows, side, width)


def call(kernel, name, outs, *operands, scalar=None, scratch=(), work=0):
    given = operands if scalar is None else (scalar, *operands)
    return pl.pallas_call(
        kernel,
        in_specs=[SMEM] * (scalar is not None) + [VMEM] * len(operands),
        out_specs=[VMEM] * len(outs),
        out_shape=[jax.ShapeDtypeStruct(*out) for out in outs],
        scratch_shapes=[pltpu.VMEM(*one) for one in scratch],
        compiler_params=PARAMS,
        cost_estimate=pl.CostEstimate(flops=work, bytes_accessed=work // 100, transcendentals=0),
        name=name,
    )(*given)


def body(pair, residue_mask, norm_gain, norm_bias, edge_w, edge_bias, out_w, out_bias):
    rows, side, width = pair.shape
    hidden = out_w.shape[1]
    dap = lax.axis_size("dap")
    chips = dap // 2
    me = lax.axis_index("dap").reshape(1)
    mask = residue_mask.reshape(1, side)
    height = 2 * rows
    count = height * side
    span = count + height * height
    half = chips // 2
    quarter = half // 2

    near = [n for n in range(half) if n % 4 in (1, 2)]
    far = [half + n for n in range(half - 2, -1, -2)]
    slots = list(zip(near, far))
    slots += [(a ^ 2, b ^ 1) for a, b in slots]
    groups = (list(range(quarter)), list(range(half - 1, quarter, -1)))
    last = quarter

    def swap(piece, distances):
        pairs = [(device, device ^ 2 * distances[device & 1]) for device in range(dap)]
        return lax.ppermute(piece, "dap", pairs)

    def flip(value):
        return lax.ppermute(value, "dap", [(device, device ^ 1) for device in range(dap)])

    def gather(own):
        pieces = [swap(own, distances) for distances in slots[:quarter]]
        return pieces + [swap(piece, (2, 1)) for piece in pieces]

    arguments = (pair, norm_gain, norm_bias, mask, edge_w, edge_bias, out_w, out_bias)
    *kept, normed = pl.pallas_call(
        load_kernel,
        in_specs=[pl.BlockSpec(memory_space=pltpu.HBM)] * len(arguments),
        out_specs=[VMEM] * (len(arguments) + 1),
        out_shape=[jax.ShapeDtypeStruct(value.shape, value.dtype) for value in arguments]
        + [jax.ShapeDtypeStruct((rows * side, width), BF16)],
        scratch_shapes=[pltpu.SemaphoreType.DMA((len(arguments),))],
        compiler_params=PARAMS,
        name="load",
    )(*[pltpu.with_memory_space_constraint(value, pltpu.HBM) for value in arguments])
    other = flip(pair)
    pair, norm_gain, norm_bias, mask, edge_w, edge_bias, out_w, out_bias = kept
    norms = (norm_gain, norm_bias)
    weights = (mask, edge_w, edge_bias)
    part_shape = (height, height, hidden)
    x_shape = (rows, side, hidden)

    both, normed = call(
        norm_kernel, "norm", [((height, side, width), F32), ((count, width), BF16)],
        pair, normed, other, *norms, scalar=me,
    )
    pieces = gather(normed)
    others, parts = [], []
    for group in groups:
        held = [slots[n] for n in group]
        outs = [((len(held), count, hidden), BF16), ((len(held), *part_shape), F32)]
        if not parts:
            outs += [((count, hidden), F32), ((count, width), F32)]
        right, part, *rest = call(
            functools.partial(outgoing_edges_kernel, held, side), "outgoing_edges", outs,
            *[pieces[n] for n in group], *weights, left if parts else normed, scalar=me,
        )
        if rest:
            left, gate = rest
        others.append(flip(right))
        parts.append(part)
    (right,) = call(
        functools.partial(outgoing_last_kernel, slots[last], side), "outgoing_last",
        [((1, count, hidden), BF16)], pieces[last], *weights, scalar=me, work=10**10,
    )
    others.append(flip(right))
    (part,) = call(
        outgoing_kernel, "outgoing", [((half, *part_shape), F32)], left, *others[:2], right
    )
    known = [[(slots[n], True) for n in group] for group in groups]
    known.append([(slots[n], False) for n in groups[0] + groups[1]] + [(slots[last], True)])
    came = [slots[last]]
    first, normed = call(
        functools.partial(outgoing_finish_kernel, came, known), "outgoing_finish",
        [((height, side, width), F32), ((count, width), BF16)],
        others[2], *parts, part, left, gate, both, *norms, out_w, out_bias,
        scalar=me, scratch=[((height, side, hidden), F32), ((len(came), *part_shape), F32)],
    )

    pieces = gather(normed)
    others, x = [], []
    for group in groups:
        held = [slots[n] for n in group]
        outs = [((len(held), span, hidden), BF16), (x_shape, F32)]
        if not x:
            outs += [((rows * side, width), F32)]
        edge, *made = call(
            functools.partial(incoming_edges_kernel, held, side), "incoming_edges", outs,
            *[pieces[n] for n in group], *weights, *(x or [normed]),
            scalar=me, scratch=[((len(held), height * height, hidden), F32)],
        )
        if not x:
            gate = made.pop()
        others.append(flip(edge))
        x = made
    (edge,) = call(
        functools.partial(incoming_last_kernel, slots[last], side), "incoming_last",
        [((1, span, hidden), BF16)], pieces[last], *weights, scalar=me, work=10**10,
    )
    others.append(flip(edge))
    x = call(
        incoming_kernel, "incoming", [(x_shape, F32)], *x, *others[:2], edge,
        scratch=[((half, height * height, hidden), F32)],
    )
    (out,) = call(
        incoming_finish_kernel, "incoming_finish", [((rows, side, width), F32)],
        *x, others[2], first, gate, *norms, out_w, out_bias, scalar=me,
        scratch=[((1, height * height, hidden), F32), (x_shape, F32)],
    )
    return out


def solution(mesh):
    in_specs = (P(("groups", "dap"), None, None), P("groups"), P(), P(), P(), P(), P(), P())
    out_specs = P(("groups", "dap"), None, None)
    return jax.shard_map(body, mesh=mesh, in_specs=in_specs, out_specs=out_specs, check_vma=False)
```
